512 devices in a mesh: dp: 16 (over y, core), expert: 32 (over z, x).
Axes of the slice: x: 4, y: 8, z: 8, core: 2. Of those that a mesh axis runs over, the one named last changes fastest.
Arguments:
- tokens: bfloat16 [2048, 3584], P('expert', 'dp'), may hold values from -6 to 6
- expert_ids: int32 [2048, 8], P('expert'), may hold values from 0 to 31, as said below
- gate_weights: float32 [2048, 8], P('expert'), may hold values from 0.1 to 1
- w_gate: bfloat16 [32, 3584, 1024], P('expert', 'dp'), may hold values from -0.09375 to 0.09375
- w_up: bfloat16 [32, 3584, 1024], P('expert', 'dp'), may hold values from -0.09375 to 0.09375
- w_down: bfloat16 [32, 1024, 3584], P('expert', None, 'dp'), may hold values from -0.1875 to 0.1875
- cotangent: bfloat16 [2048, 3584], P('expert', 'dp'), may hold values from -6 to 6
Outputs:
- mixed: bfloat16 [2048, 3584], P('expert', 'dp')
- token_grad: bfloat16 [2048, 3584], P('expert', 'dp')
- grad_gate: bfloat16 [32, 3584, 1024], P('expert', 'dp')
- grad_up: bfloat16 [32, 3584, 1024], P('expert', 'dp')
- grad_down: bfloat16 [32, 1024, 3584], P('expert', None, 'dp')
The draws below stay inside these ranges and needn't reach their ends.
Inputs may be any that keep to these rules, and one draw needn't show every extreme that they name: `expert_ids`: each row names 8 different experts. In each aligned block of 64 rows (the rows of one device) no expert is named by more than 32 rows, and one expert, the same in every block, is named by exactly 32 rows of every block.
All inputs are finite; a program needn't handle non-finite values.
Results may differ from the reference program's by a relative error of at most 0.035.
Values may be sent and summed in bfloat16 or wider, within the bound.
No kernel may reach another device: no remote copies, remote signals or barrier semaphores. Data moves between devices by JAX's collectives and lax.ppermute only.
A program may use at most 64 MiB of HBM per device.

```python
import math
import jax
import jax.numpy as jnp
from jax import lax

D = 3584
FFW = 1024
EXPERTS = 32
TOPK = 8
TOK_DEV = 64
CAP = 32
TOKENS = 2048
N_DP = 16


def pick_from(order, position):
    return order[position]


def draw_expert_ids(key, part):
    key = jax.random.fold_in(key, 11)
    hot_key, order_key, shift_key, phase_key = jax.random.split(key, 4)
    blocks = TOKENS // TOK_DEV
    others = EXPERTS - 1
    hot_expert = jax.random.randint(hot_key, (), 0, EXPERTS)
    orders = jax.vmap(lambda block_key: jax.random.permutation(block_key, others))(jax.random.split(order_key, blocks))
    orders = (orders + (orders >= hot_expert).astype(jnp.int32)).astype(jnp.int32)
    shifts = jax.random.randint(shift_key, (blocks, 1), 0, TOK_DEV)
    phases = jax.random.randint(phase_key, (blocks, 1), 0, others)
    row_numbers = jnp.arange(TOK_DEV, dtype=jnp.int32)[None, :]
    has_hot = ((row_numbers + shifts) % TOK_DEV < CAP).astype(jnp.int32)
    window_start = (TOPK * row_numbers + phases) % others
    choice_numbers = jnp.arange(TOPK, dtype=jnp.int32)[None, None, :]
    position = (window_start[:, :, None] + choice_numbers - has_hot[:, :, None]) % others
    chosen = jax.vmap(pick_from)(orders, position)
    picked = jnp.where((choice_numbers == 0) & (has_hot[:, :, None] == 1), hot_expert, chosen)
    return picked.reshape(TOKENS, TOPK).astype(jnp.int32)


def block_scale(rng, extent, cuts, low, largest):
    level, own = 1.0, jax.random.fold_in(rng, 6)
    for dim, blocks in cuts:
        steps = jnp.exp(jax.random.uniform(jax.random.fold_in(own, dim), (blocks,), jnp.float32, low / len(cuts), largest / len(cuts)))
        level = level * jnp.repeat(steps, extent[dim] // blocks).reshape([-1 if axis == dim else 1 for axis in range(len(extent))])
    return level


def scatter_about(rng, dims, deviation, most, shards=(), held_as=jnp.bfloat16):
    array = jax.random.normal(rng, dims, jnp.float32) * deviation
    if len(shards) > 0:
        array = block_scale(rng, dims, shards, -0.22, 0.18) * array
    return jnp.clip(array, min=-most, max=most).astype(held_as)


def setup_inputs(seed: int = 0) -> dict:
    arg_keys = jax.random.split(jax.random.key(seed), 8)
    return {
        "tokens": scatter_about(arg_keys[0], (TOKENS, D), 1.0, 6.0, ((0, 32), (1, 16))),
        "expert_ids": draw_expert_ids(jax.random.fold_in(arg_keys[7], 71), 0),
        "gate_weights": jnp.clip(jnp.exp(math.log(1.0) - 2.3025851 * jax.random.uniform(arg_keys[2], (TOKENS, TOPK), jnp.float32) ** block_scale(arg_keys[2], (TOKENS, TOPK), ((0, 32),), -0.2, 0.2)), 0.1, 1.0),
        "w_gate": scatter_about(arg_keys[3], (EXPERTS, D, FFW), D ** -0.5, 0.09375, ((0, 32), (1, 16))),
        "w_up": scatter_about(arg_keys[4], (EXPERTS, D, FFW), D ** -0.5, 0.09375, ((0, 32), (1, 16))),
        "w_down": scatter_about(arg_keys[5], (EXPERTS, FFW, D), FFW ** -0.5, 0.1875, ((0, 32), (2, 16))),
        "cotangent": scatter_about(arg_keys[6], (TOKENS, D), 1.0, 6.0, ((0, 32), (1, 16))),
    }


def slot_pairs(expert_ids):
    blocks = TOKENS // TOK_DEV
    pair_count = TOK_DEV * TOPK
    flat_ids = expert_ids.reshape(blocks, pair_count).astype(jnp.int32)
    numbers = jnp.arange(EXPERTS, dtype=jnp.int32)
    onehot = (flat_ids[:, :, None] == numbers[None, None, :]).astype(jnp.int32)
    slot_rank = jnp.sum((jnp.cumsum(onehot, axis=1) - 1) * onehot, axis=2).astype(jnp.int32)
    block_index = jnp.broadcast_to(jnp.arange(blocks, dtype=jnp.int32)[:, None], (blocks, pair_count))
    pair_index = (jnp.arange(pair_count, dtype=jnp.int32)[None, :] + block_index * pair_count).astype(jnp.int32)
    table = jnp.full((EXPERTS, blocks, CAP), TOKENS * TOPK, dtype=jnp.int32)
    table = table.at[flat_ids, block_index, slot_rank].set(pair_index)
    return table.reshape(EXPERTS, blocks * CAP)


def block_product(left, right):
    rows = left.shape[0]
    cols = right.shape[1]
    left_blocks = left.astype(jnp.float32).reshape(rows, N_DP, D // N_DP)
    right_blocks = right.astype(jnp.float32).reshape(N_DP, D // N_DP, cols)
    partial_sums = jnp.einsum("rbd,bdf->brf", left_blocks, right_blocks, precision=lax.Precision.HIGHEST)
    rounded = lax.optimization_barrier(partial_sums.astype(jnp.bfloat16))
    return jnp.sum(rounded.astype(jnp.float32), axis=0)


def expert_pass(inputs):
    rows_in, rows_dy, gate_matrix, up_matrix, down_matrix = inputs
    gate_sum = block_product(rows_in, gate_matrix)
    up_sum = block_product(rows_in, up_matrix)
    logistic = jax.nn.sigmoid(gate_sum)
    hidden = (gate_sum * logistic * up_sum).astype(jnp.bfloat16)
    expert_out = jnp.dot(hidden, down_matrix, preferred_element_type=jnp.float32).astype(jnp.bfloat16)
    hidden_grad = block_product(rows_dy, down_matrix.T)
    up_grad = (hidden_grad * gate_sum * logistic).astype(jnp.bfloat16)
    gate_grad = (hidden_grad * up_sum * logistic * (1.0 + gate_sum * (1.0 - logistic))).astype(jnp.bfloat16)
    row_grad = (jnp.dot(gate_grad, gate_matrix.T, preferred_element_type=jnp.float32)
                + jnp.dot(up_grad, up_matrix.T, preferred_element_type=jnp.float32)).astype(jnp.bfloat16)
    grad_gate = jnp.dot(rows_in.T, gate_grad, preferred_element_type=jnp.float32).astype(jnp.bfloat16)
    grad_up = jnp.dot(rows_in.T, up_grad, preferred_element_type=jnp.float32).astype(jnp.bfloat16)
    grad_down = jnp.dot(hidden.T, rows_dy, preferred_element_type=jnp.float32).astype(jnp.bfloat16)
    return expert_out, row_grad, grad_gate, grad_up, grad_down


def reference(tokens, expert_ids, gate_weights, w_gate, w_up, w_down, cotangent):
    pairs = slot_pairs(expert_ids)
    token_of = (pairs // TOPK).astype(jnp.int32)
    gates_padded = jnp.concatenate([gate_weights.reshape(-1), jnp.zeros((1,), jnp.float32)])
    pair_gates = gates_padded[pairs]
    tokens_padded = jnp.concatenate([tokens, jnp.zeros((1, D), jnp.bfloat16)], axis=0)
    cot_padded = jnp.concatenate([cotangent, jnp.zeros((1, D), jnp.bfloat16)], axis=0)
    rows_in = tokens_padded[token_of]
    rows_dy = (pair_gates[:, :, None] * cot_padded[token_of].astype(jnp.float32)).astype(jnp.bfloat16)
    expert_out, row_grad, grad_gate, grad_up, grad_down = lax.map(
        expert_pass, (rows_in, rows_dy, w_gate, w_up, w_down))
    mixed = jnp.zeros((TOKENS + 1, D), jnp.float32).at[token_of].add(
        pair_gates[:, :, None] * expert_out.astype(jnp.float32))
    token_grad = jnp.zeros((TOKENS + 1, D), jnp.float32).at[token_of].add(row_grad.astype(jnp.float32))
    return (mixed[:TOKENS].astype(jnp.bfloat16), token_grad[:TOKENS].astype(jnp.bfloat16),
            grad_gate, grad_up, grad_down)
```

```python
import functools
import jax
import jax.numpy as jnp
from jax import lax
from jax.experimental import pallas as pl
from jax.experimental.pallas import tpu as pltpu
from jax.sharding import Mesh, PartitionSpec as P

EXPERTS = 32
CAP = 32
BF = jnp.bfloat16
F32 = jnp.float32
SWAP = [(0, 1), (1, 0)]


def iota(shape, dim):
    return lax.broadcasted_iota(jnp.int32, shape, dim)


def contract_first(left, right, precision=None):
    return lax.dot_general(
        left, right, (((0,), (0,)), ((), ())), preferred_element_type=F32, precision=precision
    )


def slot_table(ids, gates):
    tokens = ids.shape[0]
    numbers = iota((tokens, EXPERTS), 1)
    chosen = jnp.zeros((tokens, EXPERTS), F32)
    weight = jnp.zeros((tokens, EXPERTS), F32)
    for k in range(ids.shape[1]):
        hit = ids[:, k : k + 1] == numbers
        chosen = chosen + hit.astype(F32)
        weight = weight + jnp.where(hit, gates[:, k : k + 1], 0.0)
    row, col = iota((tokens, tokens), 0), iota((tokens, tokens), 1)
    earlier = (row < col).astype(F32)
    same = (row == col).astype(F32)
    rank_t = contract_first(chosen, earlier)
    chosen_t = contract_first(chosen, same)
    weight_t = contract_first(weight, same, lax.Precision.HIGHEST)
    code = jnp.where(chosen_t > 0.5, rank_t, -1.0).astype(jnp.int32)
    slots = iota((EXPERTS, CAP, tokens), 1)
    hit = code[:, None, :] == slots
    pick = jnp.where(hit, 1.0, 0.0).reshape(EXPERTS * CAP, tokens)
    slot_gate = jnp.sum(jnp.where(hit, weight_t[:, None, :], 0.0), axis=2, keepdims=True)
    return pick, slot_gate.reshape(EXPERTS * CAP, 1)


def send_kernel(ids_ref, gates_ref, tokens_ref, cotangent_ref, rows_ref, dy_ref):
    pick, slot_gate = slot_table(ids_ref[...], gates_ref[...])
    pick = pick.astype(BF)
    rows = jnp.dot(pick, tokens_ref[...], preferred_element_type=F32)
    rows_ref[...] = rows.astype(BF)
    dy = jnp.dot(pick, cotangent_ref[...], preferred_element_type=F32)
    dy_ref[...] = (dy * slot_gate).astype(BF)


def mix_kernel(ids_ref, gates_ref, back_ref, mixed_ref):
    pick, slot_gate = slot_table(ids_ref[...], gates_ref[...])
    pick = pick.astype(BF)
    scaled = back_ref[...].astype(F32) * slot_gate
    high = scaled.astype(BF)
    low = (scaled - high.astype(F32)).astype(BF)
    mixed_ref[...] = (contract_first(pick, high) + contract_first(pick, low)).astype(BF)


def grad_kernel(ids_ref, gates_ref, back_ref, grad_ref):
    pick, _ = slot_table(ids_ref[...], gates_ref[...])
    grad_ref[...] = contract_first(pick.astype(BF), back_ref[...]).astype(BF)


def dot(spec, left, right):
    return jnp.einsum(spec, left, right, preferred_element_type=F32)


def to_experts(rows):
    width = rows.shape[1]
    rows = rows.reshape(EXPERTS, CAP, width)
    rows = lax.all_to_all(rows, "expert", split_axis=0, concat_axis=0, tiled=True)
    return rows.reshape(EXPERTS * CAP, width)


def halves(rows, core):
    rows = rows.reshape(8, 2, 64, rows.shape[1])
    own = lax.dynamic_index_in_dim(rows, core, 1, keepdims=False)
    other = lax.dynamic_index_in_dim(rows, 1 - core, 1, keepdims=False)
    return own.reshape(512, -1), other.reshape(512, -1)


def scatter(part):
    return lax.psum_scatter(part, "y", scatter_dimension=0, tiled=True).astype(F32)


def gather(shard):
    return lax.all_gather(shard, ("y", "core"), axis=0, tiled=True)


def body(tokens, expert_ids, gate_weights, w_gate, w_up, w_down, cotangent):
    width = tokens.shape[1]
    slots = EXPERTS * CAP
    w_gate, w_up, w_down = w_gate[0], w_up[0], w_down[0]
    core = lax.axis_index("core")
    send_in, send_dy = pl.pallas_call(
        send_kernel,
        out_shape=[jax.ShapeDtypeStruct((slots, width), BF)] * 2,
        name="send_rows",
    )(expert_ids, gate_weights, tokens, cotangent)
    rows_in = to_experts(send_in)
    rows_dy = to_experts(send_dy)

    own, other = halves(rows_in, core)
    gate_other = lax.ppermute(dot("rd,df->rf", other, w_gate).astype(BF), "core", SWAP)
    up_other = lax.ppermute(dot("rd,df->rf", other, w_up).astype(BF), "core", SWAP)
    gate_part = (dot("rd,df->rf", own, w_gate) + gate_other.astype(F32)).astype(BF)
    up_part = (dot("rd,df->rf", own, w_up) + up_other.astype(F32)).astype(BF)
    gate_sum = scatter(gate_part)
    up_sum = scatter(up_part)

    own, other = halves(rows_dy, core)
    hid_other = lax.ppermute(dot("rd,fd->rf", other, w_down).astype(BF), "core", SWAP)
    hid_part = (dot("rd,fd->rf", own, w_down) + hid_other.astype(F32)).astype(BF)
    hidden_grad = scatter(hid_part)

    logistic = jax.nn.sigmoid(gate_sum)
    hidden = gather((gate_sum * logistic * up_sum).astype(BF))
    up_grad = (hidden_grad * gate_sum * logistic).astype(BF)
    gate_grad = (hidden_grad * up_sum * logistic * (1.0 + gate_sum * (1.0 - logistic))).astype(BF)
    up_grad = gather(up_grad)
    gate_grad = gather(gate_grad)

    out_rows = dot("rf,fd->rd", hidden, w_down).astype(BF)
    back_out = to_experts(out_rows)
    mixed = pl.pallas_call(
        mix_kernel, out_shape=jax.ShapeDtypeStruct(tokens.shape, BF), name="mix_rows"
    )(expert_ids, gate_weights, back_out)

    row_grad = (
        dot("rf,df->rd", gate_grad, w_gate) + dot("rf,df->rd", up_grad, w_up)
    ).astype(BF)
    back_grad = to_experts(row_grad)
    token_grad = pl.pallas_call(
        grad_kernel, out_shape=jax.ShapeDtypeStruct(tokens.shape, BF), name="sum_rows"
    )(expert_ids, gate_weights, back_grad)

    grad_down = dot("rf,rd->fd", hidden, rows_dy).astype(BF)
    grad_gate = dot("rd,rf->df", rows_in, gate_grad).astype(BF)
    grad_up = dot("rd,rf->df", rows_in, up_grad).astype(BF)
    return mixed, token_grad, grad_gate[None], grad_up[None], grad_down[None]


def solution(mesh):
    fine = Mesh(mesh.devices.reshape(8, 2, 32), ("y", "core", "expert"))
    dp = ("y", "core")
    placed = (
        P("expert", dp),
        P("expert", None),
        P("expert", None),
        P("expert", dp, None),
        P("expert", dp, None),
        P("expert", None, dp),
        P("expert", dp),
    )
    return jax.shard_map(
        body,
        mesh=fine,
        in_specs=placed,
        out_specs=(
            P("expert", dp),
            P("expert", dp),
            P("expert", dp, None),
            P("expert", dp, None),
            P("expert", None, dp),
        ),
        check_vma=False,
    )
```

```python
import jax
import jax.numpy as jnp
from jax import lax
from jax.experimental import pallas as pl
from jax.experimental.pallas import tpu as pltpu
from jax.sharding import Mesh, PartitionSpec as P

EXPERTS = 32
CAP = 32
HALF = CAP // 2
ROWS = EXPERTS * HALF
WIDE = 224
FFW = 1024
OWN = slice(0, WIDE)
OTHER = slice(256, 256 + WIDE)
BOTH = 512
STEP = 128
N_Y = 8
BF = jnp.bfloat16
F32 = jnp.float32


def iota(shape, dim):
    return lax.broadcasted_iota(jnp.int32, shape, dim)


def dot(left, right):
    return jnp.dot(left, right, preferred_element_type=F32)


def dot_t(left, right):
    return lax.dot_general(left, right, (((1,), (1,)), ((), ())), preferred_element_type=F32)


def t_dot(left, right):
    return lax.dot_general(left, right, (((0,), (0,)), ((), ())), preferred_element_type=F32)


def shape(*dims, dtype=BF):
    return jax.ShapeDtypeStruct(dims, dtype)


def table_kernel(core_ref, ids_ref, gates_ref, pick_ref, gate_ref):
    tokens = ids_ref.shape[1]
    numbers = iota((EXPERTS, tokens), 0)
    chosen = jnp.zeros((EXPERTS, tokens), F32)
    weight = jnp.zeros((EXPERTS, tokens), F32)
    for k in range(ids_ref.shape[0]):
        hit = ids_ref[k : k + 1, :] == numbers
        chosen = chosen + jnp.where(hit, 1.0, 0.0)
        weight = weight + jnp.where(hit, gates_ref[k : k + 1, :], 0.0)
    earlier = jnp.where(iota((tokens, tokens), 0) < iota((tokens, tokens), 1), 1.0, 0.0)
    rank = dot(chosen.astype(BF), earlier.astype(BF))
    slot = jnp.where(chosen > 0.5, rank, -1.0).astype(jnp.int32) - core_ref[0] * HALF
    hit = slot[:, None, :] == iota((EXPERTS, HALF, tokens), 1)
    pick_ref[...] = jnp.where(hit, 1.0, 0.0).reshape(ROWS, tokens).astype(BF)
    gate = jnp.sum(jnp.where(hit, weight[:, None, :], 0.0), axis=2, keepdims=True)
    gate_ref[...] = gate.reshape(ROWS, 1)


def rows_kernel(pick_ref, own_ref, other_ref, out_ref):
    out_ref[...] = jnp.zeros_like(out_ref)
    out_ref[:, OWN] = dot(pick_ref[...], own_ref[...]).astype(BF)
    out_ref[:, OTHER] = dot(pick_ref[...], other_ref[...]).astype(BF)


def scaled_kernel(pick_ref, gate_ref, own_ref, other_ref, out_ref):
    out_ref[...] = jnp.zeros_like(out_ref)
    out_ref[:, OWN] = (dot(pick_ref[...], own_ref[...]) * gate_ref[...]).astype(BF)
    out_ref[:, OTHER] = (dot(pick_ref[...], other_ref[...]) * gate_ref[...]).astype(BF)


def gate_up_kernel(rows_ref, gate_own, gate_other, up_own, up_other, out_ref):
    own, other = rows_ref[:, OWN], rows_ref[:, OTHER]
    out_ref[:, :FFW] = (dot(own, gate_own[...]) + dot(other, gate_other[...])).astype(BF)
    out_ref[:, FFW:] = (dot(own, up_own[...]) + dot(other, up_other[...])).astype(BF)


def hidden_grad_kernel(dy_ref, down_own, down_other, out_ref):
    own, other = dy_ref[:, OWN], dy_ref[:, OTHER]
    out_ref[...] = (dot_t(own, down_own[...]) + dot_t(other, down_other[...])).astype(BF)


def out_kernel(hidden_ref, down_own, down_other, out_ref):
    out_ref[...] = jnp.zeros_like(out_ref)
    out_ref[:, OWN] = dot(hidden_ref[...], down_own[...]).astype(BF)
    out_ref[:, OTHER] = dot(hidden_ref[...], down_other[...]).astype(BF)


def row_grad_kernel(grads_ref, gate_own, gate_other, up_own, up_other, out_ref):
    gate, up = grads_ref[:, :FFW], grads_ref[:, FFW:]
    out_ref[...] = jnp.zeros_like(out_ref)
    out_ref[:, OWN] = (dot_t(gate, gate_own[...]) + dot_t(up, up_own[...])).astype(BF)
    out_ref[:, OTHER] = (dot_t(gate, gate_other[...]) + dot_t(up, up_other[...])).astype(BF)


def mix_kernel(pick_ref, gate_ref, back_ref, own_ref, other_ref):
    scaled = back_ref[...].astype(F32) * gate_ref[...]
    high = scaled.astype(BF)
    low = (scaled - high.astype(F32)).astype(BF)
    total = t_dot(pick_ref[...], high) + t_dot(pick_ref[...], low)
    own_ref[...] = total[:, OWN]
    other_ref[...] = total[:, OTHER]


def sum_kernel(pick_ref, back_ref, own_ref, other_ref):
    total = t_dot(pick_ref[...], back_ref[...])
    own_ref[...] = total[:, OWN]
    other_ref[...] = total[:, OTHER]


def per_rows(kernel, out_width, rows, *weights):
    whole = [pl.BlockSpec(w.shape, lambda i: (0, 0)) for w in weights]
    return pl.pallas_call(
        kernel,
        grid=(ROWS // STEP,),
        in_specs=[pl.BlockSpec((STEP, rows.shape[1]), lambda i: (i, 0))] + whole,
        out_specs=pl.BlockSpec((STEP, out_width), lambda i: (i, 0)),
        out_shape=shape(ROWS, out_width),
        compiler_params=pltpu.CompilerParams(vmem_limit_bytes=32 * 1024 * 1024),
        name=kernel.__name__,
    )(rows, *weights)


def at_once(kernel, out_shape, *args):
    return pl.pallas_call(
        kernel,
        out_shape=out_shape,
        compiler_params=pltpu.CompilerParams(vmem_limit_bytes=32 * 1024 * 1024),
        name=kernel.__name__,
    )(*args)


def to_experts(rows):
    rows = rows.reshape(EXPERTS, HALF, rows.shape[1])
    rows = lax.all_to_all(rows, "expert", split_axis=0, concat_axis=0, tiled=True)
    return rows.reshape(ROWS, -1)


def across(parts):
    return lax.all_to_all(parts, "y", split_axis=0, concat_axis=0, tiled=True)


def swap(array):
    return lax.ppermute(array, "core", [(0, 1), (1, 0)])


def after(array, *others):
    return lax.optimization_barrier((array,) + others)[0]


def body(tokens, expert_ids, gate_weights, w_gate, w_up, w_down, cotangent):
    gate_own, up_own, down_own = w_gate[0], w_up[0], w_down[0]
    core = lax.axis_index("core").reshape(1)
    tokens_other, cotangent_other = swap(tokens), swap(cotangent)
    pick, slot_gate = pl.pallas_call(
        table_kernel,
        in_specs=[pl.BlockSpec(memory_space=pltpu.SMEM)]
        + [pl.BlockSpec(memory_space=pltpu.VMEM)] * 2,
        out_shape=[shape(ROWS, tokens.shape[0]), shape(ROWS, 1, dtype=F32)],
        name="table_kernel",
    )(core, expert_ids.T, gate_weights.T)

    send_in = at_once(rows_kernel, shape(ROWS, BOTH), pick, tokens, tokens_other)
    gate_other = swap(after(gate_own, send_in))
    up_other = swap(after(up_own, send_in))
    down_other = swap(after(down_own, send_in))
    rows_in = to_experts(send_in)
    send_dy = at_once(
        scaled_kernel, shape(ROWS, BOTH), pick, slot_gate, cotangent, cotangent_other
    )
    rows_dy = to_experts(after(send_dy, rows_in))

    gate_up = per_rows(gate_up_kernel, 2 * FFW, rows_in, gate_own, gate_other, up_own, up_other)
    sums = lax.psum_scatter(gate_up, "y", scatter_dimension=0, tiled=True).astype(F32)
    rows_dy = after(rows_dy, gate_up)
    parts = per_rows(hidden_grad_kernel, FFW, rows_dy, down_own, down_other)
    parts = across(parts.reshape(N_Y, ROWS // N_Y, FFW))
    hidden_grad = jnp.sum(parts.astype(F32), axis=0)

    gate_sum, up_sum = sums[:, :FFW], sums[:, FFW:]
    logistic = jax.nn.sigmoid(gate_sum)
    hidden = (gate_sum * logistic * up_sum).astype(BF)
    up_grad = (hidden_grad * gate_sum * logistic).astype(BF)
    gate_grad = (hidden_grad * up_sum * logistic * (1.0 + gate_sum * (1.0 - logistic))).astype(BF)
    shard = jnp.concatenate([gate_grad, up_grad], axis=1)
    grads = lax.all_gather(shard, "y", axis=0, tiled=True)
    hidden = across(jnp.broadcast_to(after(hidden, shard), (N_Y,) + hidden.shape))
    hidden = hidden.reshape(ROWS, FFW)

    out_rows = per_rows(out_kernel, BOTH, hidden, down_own, down_other)
    back_out = to_experts(out_rows)
    part_shape = [shape(*tokens.shape, dtype=F32)] * 2
    mixed, mixed_other = at_once(mix_kernel, part_shape, pick, slot_gate, back_out)
    mixed = (mixed + swap(mixed_other)).astype(BF)

    row_grad = per_rows(row_grad_kernel, BOTH, grads, gate_own, gate_other, up_own, up_other)
    back_grad = to_experts(row_grad)

    down_part = swap(t_dot(hidden, rows_dy[:, OTHER]).astype(BF))
    grad_down = (t_dot(hidden, rows_dy[:, OWN]) + down_part.astype(F32)).astype(BF)
    gate_part = swap(t_dot(rows_in[:, OTHER], grads[:, :FFW]).astype(BF))
    up_part = swap(t_dot(rows_in[:, OTHER], grads[:, FFW:]).astype(BF))
    grad_gate = (t_dot(rows_in[:, OWN], grads[:, :FFW]) + gate_part.astype(F32)).astype(BF)
    grad_up = (t_dot(rows_in[:, OWN], grads[:, FFW:]) + up_part.astype(F32)).astype(BF)

    token_grad, grad_other = at_once(sum_kernel, part_shape, pick, back_grad)
    token_grad = (token_grad + swap(grad_other)).astype(BF)
    return mixed, token_grad, grad_gate[None], grad_up[None], grad_down[None]


def solution(mesh):
    fine = Mesh(mesh.devices.reshape(N_Y, 2, EXPERTS), ("y", "core", "expert"))
    dp = ("y", "core")
    placed = (
        P("expert", dp),
        P("expert", None),
        P("expert", None),
        P("expert", dp, None),
        P("expert", dp, None),
        P("expert", None, dp),
        P("expert", dp),
    )
    return jax.shard_map(
        body,
        mesh=fine,
        in_specs=placed,
        out_specs=(
            P("expert", dp),
            P("expert", dp),
            P("expert", dp, None),
            P("expert", dp, None),
            P("expert", None, dp),
        ),
        check_vma=False,
    )
```

```python
import jax
import jax.numpy as jnp
from jax import lax
from jax.experimental import pallas as pl
from jax.experimental.pallas import tpu as pltpu
from jax.sharding import Mesh, PartitionSpec as P

EXPERTS = 32
CAP = 32
HALF = CAP // 2
ROWS = EXPERTS * HALF
WIDE = 224
PAIR = 2 * WIDE
STACK = 512
JOIN = 2 * PAIR - STACK
FFW = 1024
N_Y = 8
SHARD = ROWS // N_Y
BF = jnp.bfloat16
F32 = jnp.float32
VMEM_LIMIT = 24 * 1024 * 1024


def iota(shape, dim):
    return lax.broadcasted_iota(jnp.int32, shape, dim)


def dot(left, right):
    return jnp.dot(left, right, preferred_element_type=F32)


def dot_t(left, right):
    return lax.dot_general(left, right, (((1,), (1,)), ((), ())), preferred_element_type=F32)


def t_dot(left, right):
    return lax.dot_general(left, right, (((0,), (0,)), ((), ())), preferred_element_type=F32)


def shape(*dims, dtype=BF):
    return jax.ShapeDtypeStruct(dims, dtype)


def start(copies):
    for copy in copies:
        copy.start()


def wait(copies):
    for copy in copies:
        copy.wait()


def copies_of(pairs, sems):
    return [pltpu.make_async_copy(src, dst, sems.at[i]) for i, (src, dst) in enumerate(pairs)]


def send_kernel(
    core_ref,
    ids_hbm,
    gates_hbm,
    tokens_hbm,
    cotangent_hbm,
    others_hbm,
    pick_ref,
    gate_ref,
    out_ref,
    ids_ref,
    gates_ref,
    tokens_ref,
    cotangent_ref,
    others_ref,
    sems,
):
    loads = copies_of(
        (
            (ids_hbm, ids_ref),
            (gates_hbm, gates_ref),
            (tokens_hbm, tokens_ref),
            (cotangent_hbm, cotangent_ref),
            (others_hbm, others_ref),
        ),
        sems,
    )
    start(loads)
    wait(loads[:2])
    tokens = ids_ref.shape[1]
    numbers = iota((EXPERTS, tokens), 0)
    chosen = jnp.zeros((EXPERTS, tokens), F32)
    weight = jnp.zeros((EXPERTS, tokens), F32)
    for k in range(ids_ref.shape[0]):
        hit = ids_ref[k : k + 1, :] == numbers
        chosen = chosen + jnp.where(hit, 1.0, 0.0)
        weight = weight + jnp.where(hit, gates_ref[k : k + 1, :], 0.0)
    earlier = jnp.where(iota((tokens, tokens), 0) < iota((tokens, tokens), 1), 1.0, 0.0)
    rank = dot(chosen.astype(BF), earlier.astype(BF))
    slot = jnp.where(chosen > 0.5, rank, -1.0).astype(jnp.int32) - core_ref[0] * HALF
    hit = slot[:, None, :] == iota((EXPERTS, HALF, tokens), 1)
    pick = jnp.where(hit, 1.0, 0.0).reshape(ROWS, tokens).astype(BF)
    gate = jnp.sum(jnp.where(hit, weight[:, None, :], 0.0), axis=2, keepdims=True)
    gate = gate.reshape(ROWS, 1)
    pick_ref[...] = pick
    gate_ref[...] = gate
    wait(loads[2:])
    features = jnp.concatenate(
        [tokens_ref[...], others_ref[:tokens], cotangent_ref[...], others_ref[tokens:]], axis=1
    )
    rows = dot(pick, features)
    scale = jnp.where(iota((1, 2 * PAIR), 1) < PAIR, 1.0, gate)
    out_ref[...] = (rows * scale).astype(BF)


def sums_kernel(rows, gate, up, down, out_hbm, out, sems):
    columns = [pl.ds(i * FFW, FFW) for i in range(3)]
    stores = copies_of([(out.at[:, c], out_hbm.at[:, c]) for c in columns], sems)
    for i, weights in enumerate((gate, up, down)):
        left = rows[:, :STACK] if i < 2 else rows[:, 2 * PAIR - STACK :]
        out[:, i * FFW : (i + 1) * FFW] = dot(left, weights[...]).astype(BF)
        stores[i].start()
    wait(stores)


def shard_kernel(sums_hbm, out_hbm, sums, out, in_sems, out_sems):
    columns = [pl.ds(i * FFW, FFW) for i in range(3)]
    loads = copies_of([(sums_hbm.at[:, c], sums.at[:, c]) for c in columns], in_sems)
    stores = copies_of([(out.at[:, c], out_hbm.at[:, c]) for c in columns], out_sems)
    start(loads)
    wait(loads[:2])
    gate_sum = sums[:, :FFW].astype(F32)
    up_sum = sums[:, FFW : 2 * FFW].astype(F32)
    logistic = jax.nn.sigmoid(gate_sum)
    silu = gate_sum * logistic
    out[:, :FFW] = (silu * up_sum).astype(BF)
    stores[0].start()
    loads[2].wait()
    total = sums[:, 2 * FFW :].astype(F32)
    slope = logistic * (1.0 + gate_sum * (1.0 - logistic))
    out[:, FFW : 2 * FFW] = (total * up_sum * slope).astype(BF)
    stores[1].start()
    out[:, 2 * FFW :] = (total * silu).astype(BF)
    stores[2].start()
    wait(stores)


def back_kernel(full_hbm, gate, up, down, out_hbm, full, out, in_sems, out_sems):
    half = ROWS // 2
    parts = [pl.ds(i * half, half) for i in range(2)]
    columns = [pl.ds(i * FFW, FFW) for i in range(3)]
    blocks = [(p, c) for p in parts for c in columns]
    loads = copies_of([(full_hbm.at[p, c], full.at[p, c]) for p, c in blocks], in_sems)
    stores = copies_of([(out.at[p], out_hbm.at[p]) for p in parts], out_sems)
    start(loads)
    for i in range(2):
        rows = slice(i * half, (i + 1) * half)
        loads[3 * i].wait()
        result = dot_t(full[rows, :FFW], down[...])
        loads[3 * i + 1].wait()
        grad = dot_t(full[rows, FFW : 2 * FFW], gate[...])
        loads[3 * i + 2].wait()
        grad = grad + dot_t(full[rows, 2 * FFW :], up[...])
        out[rows, :JOIN] = grad[:, :JOIN].astype(BF)
        out[rows, JOIN:STACK] = (grad[:, JOIN:] + result[:, : STACK - JOIN]).astype(BF)
        out[rows, STACK:] = result[:, STACK - JOIN :].astype(BF)
        stores[i].start()
    wait(stores)


def mix_kernel(pick_ref, gate_ref, back_ref, out_ref):
    scaled = back_ref[:, JOIN:].astype(F32) * gate_ref[...]
    high = scaled.astype(BF)
    low = (scaled - high.astype(F32)).astype(BF)
    mixed = t_dot(pick_ref[...], high) + t_dot(pick_ref[...], low)
    grad = t_dot(pick_ref[...], back_ref[:, :STACK])
    out_ref[:, :JOIN] = grad[:, :JOIN]
    first = iota((1, STACK - JOIN), 1) < PAIR - JOIN
    out_ref[:, JOIN:STACK] = jnp.where(first, grad[:, JOIN:], mixed[:, : STACK - JOIN])
    out_ref[:, STACK:] = mixed[:, STACK - JOIN :]


HBM_SPEC = pl.BlockSpec(memory_space=pltpu.HBM)
VMEM_SPEC = pl.BlockSpec(memory_space=pltpu.VMEM)
SMEM_SPEC = pl.BlockSpec(memory_space=pltpu.SMEM)


def call(kernel, out_shape, *args, **kwargs):
    return pl.pallas_call(
        kernel,
        out_shape=out_shape,
        compiler_params=pltpu.CompilerParams(vmem_limit_bytes=VMEM_LIMIT),
        name=kernel.__name__,
        **kwargs,
    )(*args)


def in_hbm(*arrays):
    return [pltpu.with_memory_space_constraint(a, pltpu.HBM) for a in arrays]


def in_vmem(*arrays):
    return [pltpu.with_memory_space_constraint(a, pltpu.VMEM) for a in arrays]


def buffers(*arrays):
    return [pltpu.VMEM(a.shape, a.dtype) for a in arrays]


def semaphores(*counts):
    return [pltpu.SemaphoreType.DMA((n,)) for n in counts]


def to_experts(rows):
    rows = rows.reshape(EXPERTS, HALF, rows.shape[1])
    rows = lax.all_to_all(rows, "expert", split_axis=0, concat_axis=0, tiled=True)
    return rows.reshape(ROWS, -1)


def swap(array):
    return lax.ppermute(array, "core", [(0, 1), (1, 0)])


def after(array, *others):
    return lax.optimization_barrier((array,) + others)[0]


def body(tokens, expert_ids, gate_weights, w_gate, w_up, w_down, cotangent):
    gate_own, up_own, down_own = w_gate[0], w_up[0], w_down[0].T
    others = swap(jnp.concatenate([tokens, cotangent], axis=0))
    inputs = (expert_ids.T, gate_weights.T, tokens, cotangent, others)
    pick, slot_gate, send = call(
        send_kernel,
        [shape(ROWS, tokens.shape[0]), shape(ROWS, 1, dtype=F32), shape(ROWS, 2 * PAIR)],
        lax.axis_index("core").reshape(1),
        *in_hbm(*inputs),
        in_specs=[SMEM_SPEC] + [HBM_SPEC] * 5,
        scratch_shapes=buffers(*inputs) + semaphores(5),
    )
    rows = to_experts(send)
    gate_own, up_own, down_own, _ = lax.optimization_barrier((gate_own, up_own, down_own, send))
    zeros = jnp.zeros((STACK - PAIR, FFW), BF)
    gate_stack = jnp.concatenate([gate_own, swap(gate_own), zeros], axis=0)
    up_stack = jnp.concatenate([up_own, swap(up_own), zeros], axis=0)
    down_stack = jnp.concatenate([zeros, down_own, swap(down_own)], axis=0)

    parts = call(
        sums_kernel,
        shape(ROWS, 3 * FFW),
        rows,
        *in_vmem(gate_stack, up_stack, down_stack),
        in_specs=[VMEM_SPEC] * 4,
        out_specs=HBM_SPEC,
        scratch_shapes=[pltpu.VMEM((ROWS, 3 * FFW), BF)] + semaphores(3),
    )
    sums = lax.psum_scatter(parts, "y", scatter_dimension=0, tiled=True)
    shard = call(
        shard_kernel,
        shape(SHARD, 3 * FFW),
        *in_hbm(sums),
        in_specs=[HBM_SPEC],
        out_specs=HBM_SPEC,
        scratch_shapes=buffers(sums, sums) + semaphores(3, 3),
    )
    full = lax.all_gather(shard, "y", axis=0, tiled=True)
    back = call(
        back_kernel,
        shape(ROWS, 2 * PAIR),
        *in_hbm(full),
        *in_vmem(gate_stack, up_stack, down_stack),
        in_specs=[HBM_SPEC] + [VMEM_SPEC] * 3,
        out_specs=HBM_SPEC,
        scratch_shapes=buffers(full, rows) + semaphores(6, 2),
    )
    back = to_experts(back)

    in_own, in_other = rows[:, :WIDE], rows[:, WIDE:PAIR]
    dy_own, dy_other = rows[:, PAIR : PAIR + WIDE], rows[:, PAIR + WIDE :]
    hidden, gate_grad, up_grad = full[:, :FFW], full[:, FFW : 2 * FFW], full[:, 2 * FFW :]
    down_part = swap(t_dot(dy_other, hidden).astype(BF)).astype(F32)
    part = swap(t_dot(in_other, full[:, FFW:]).astype(BF)).astype(F32)
    grad_down = (t_dot(dy_own, hidden) + down_part).astype(BF).T
    grad_gate = (t_dot(in_own, gate_grad) + part[:, :FFW]).astype(BF)
    grad_up = (t_dot(in_own, up_grad) + part[:, FFW:]).astype(BF)

    back = after(back, grad_down, grad_gate, grad_up)
    total = call(mix_kernel, shape(tokens.shape[0], 2 * PAIR, dtype=F32), pick, slot_gate, back)
    other = swap(total)
    token_grad = (total[:, :WIDE] + other[:, WIDE:PAIR]).astype(BF)
    mixed = (total[:, PAIR : PAIR + WIDE] + other[:, PAIR + WIDE :]).astype(BF)
    return mixed, token_grad, grad_gate[None], grad_up[None], grad_down[None]


def solution(mesh):
    fine = Mesh(mesh.devices.reshape(N_Y, 2, EXPERTS), ("y", "core", "expert"))
    dp = ("y", "core")
    placed = (
        P("expert", dp),
        P("expert", None),
        P("expert", None),
        P("expert", dp, None),
        P("expert", dp, None),
        P("expert", None, dp),
        P("expert", dp),
    )
    return jax.shard_map(
        body,
        mesh=fine,
        in_specs=placed,
        out_specs=(
            P("expert", dp),
            P("expert", dp),
            P("expert", dp, None),
            P("expert", dp, None),
            P("expert", None, dp),
        ),
        check_vma=False,
    )
```

```python
import jax
import jax.numpy as jnp
from jax import lax
from jax.experimental import pallas as pl
from jax.experimental.pallas import tpu as pltpu
from jax.sharding import Mesh, PartitionSpec as P

EXPERTS = 32
CAP = 32
HALF = CAP // 2
ROWS = EXPERTS * HALF
WIDE = 224
PAIR = 2 * WIDE
STACK = 512
JOIN = 2 * PAIR - STACK
FFW = 1024
N_Y = 8
SHARD = ROWS // N_Y
BF = jnp.bfloat16
F32 = jnp.float32
VMEM_LIMIT = 24 * 1024 * 1024


def iota(shape, dim):
    return lax.broadcasted_iota(jnp.int32, shape, dim)


def dot(left, right):
    return jnp.dot(left, right, preferred_element_type=F32)


def dot_t(left, right):
    return lax.dot_general(left, right, (((1,), (1,)), ((), ())), preferred_element_type=F32)


def t_dot(left, right):
    return lax.dot_general(left, right, (((0,), (0,)), ((), ())), preferred_element_type=F32)


def shape(*dims, dtype=BF):
    return jax.ShapeDtypeStruct(dims, dtype)


def start(copies):
    for copy in copies:
        copy.start()


def wait(copies):
    for copy in copies:
        copy.wait()


def copies_of(pairs, sems):
    return [pltpu.make_async_copy(src, dst, sems.at[i]) for i, (src, dst) in enumerate(pairs)]


def slot_table(ids_ref, gates_ref, first):
    tokens = ids_ref.shape[1]
    numbers = iota((EXPERTS, tokens), 0)
    chosen = jnp.zeros((EXPERTS, tokens), F32)
    weight = jnp.zeros((EXPERTS, tokens), F32)
    for k in range(ids_ref.shape[0]):
        hit = ids_ref[k : k + 1, :] == numbers
        chosen = chosen + jnp.where(hit, 1.0, 0.0)
        weight = weight + jnp.where(hit, gates_ref[k : k + 1, :], 0.0)
    earlier = jnp.where(iota((tokens, tokens), 0) < iota((tokens, tokens), 1), 1.0, 0.0)
    rank = dot(chosen.astype(BF), earlier.astype(BF))
    slot = jnp.where(chosen > 0.5, rank, -1.0).astype(jnp.int32) - first
    hit = slot[:, None, :] == iota((EXPERTS, HALF, tokens), 1)
    pick = jnp.where(hit, 1.0, 0.0).reshape(ROWS, tokens).astype(BF)
    gate = jnp.sum(jnp.where(hit, weight[:, None, :], 0.0), axis=2, keepdims=True)
    return pick, gate.reshape(ROWS, 1)


def send_kernel(
    core_ref,
    others_ref,
    ids_hbm,
    gates_hbm,
    tokens_hbm,
    cotangent_hbm,
    out_ref,
    ids_ref,
    gates_ref,
    tokens_ref,
    cotangent_ref,
    sems,
):
    loads = copies_of(
        (
            (ids_hbm, ids_ref),
            (gates_hbm, gates_ref),
            (tokens_hbm, tokens_ref),
            (cotangent_hbm, cotangent_ref),
        ),
        sems,
    )
    start(loads)
    wait(loads[:2])
    pick, gate = slot_table(ids_ref, gates_ref, core_ref[0] * HALF)
    wait(loads[2:])
    count = tokens_ref.shape[0]
    features = jnp.concatenate(
        [tokens_ref[...], others_ref[:count], cotangent_ref[...], others_ref[count:]], axis=1
    )
    rows = dot(pick, features)
    scale = jnp.where(iota((1, 2 * PAIR), 1) < PAIR, 1.0, gate)
    out_ref[...] = (rows * scale).astype(BF)


def table_kernel(ids_ref, gates_ref, pick_ref, gate_ref):
    for half in range(2):
        pick_ref[half], gate_ref[half] = slot_table(ids_ref, gates_ref, half * HALF)


def sums_kernel(rows, gate, up, down, out_hbm, out, sems):
    columns = [pl.ds(i * FFW, FFW) for i in range(3)]
    stores = copies_of([(out.at[:, c], out_hbm.at[:, c]) for c in columns], sems)
    for i, weights in enumerate((gate, up, down)):
        left = rows[:, :STACK] if i < 2 else rows[:, 2 * PAIR - STACK :]
        out[:, i * FFW : (i + 1) * FFW] = dot(left, weights[...]).astype(BF)
        stores[i].start()
    wait(stores)


def shard_kernel(sums_hbm, out_hbm, sums, out, in_sems, out_sems):
    columns = [pl.ds(i * FFW, FFW) for i in range(3)]
    loads = copies_of([(sums_hbm.at[:, c], sums.at[:, c]) for c in columns], in_sems)
    stores = copies_of([(out.at[:, c], out_hbm.at[:, c]) for c in columns], out_sems)
    start(loads)
    wait(loads[:2])
    gate_sum = sums[:, :FFW].astype(F32)
    up_sum = sums[:, FFW : 2 * FFW].astype(F32)
    logistic = jax.nn.sigmoid(gate_sum)
    silu = gate_sum * logistic
    out[:, :FFW] = (silu * up_sum).astype(BF)
    stores[0].start()
    loads[2].wait()
    total = sums[:, 2 * FFW :].astype(F32)
    slope = logistic * (1.0 + gate_sum * (1.0 - logistic))
    out[:, FFW : 2 * FFW] = (total * up_sum * slope).astype(BF)
    stores[1].start()
    out[:, 2 * FFW :] = (total * silu).astype(BF)
    stores[2].start()
    wait(stores)


def back_kernel(full_hbm, gate_hbm, up_hbm, down_hbm, out_ref, full, weights, sems):
    blocks = [(y, half) for y in range(N_Y) for half in range(2)]
    loads = copies_of(
        [(w, weights.at[i]) for i, w in enumerate((down_hbm, gate_hbm, up_hbm))]
        + [
            (
                full_hbm.at[pl.ds((2 * y + half) * SHARD, SHARD)],
                full.at[half, pl.ds(y * SHARD, SHARD)],
            )
            for y, half in blocks
        ],
        sems,
    )
    start(loads)
    wait(loads[:3])
    loads = loads[3:]
    step = ROWS // 2
    for i in range(2):
        wait(loads[i * N_Y : (i + 1) * N_Y])
        rows = slice(i * step, (i + 1) * step)
        parts = []
        for half in range(2):
            grad = dot_t(full[half, rows, FFW : 2 * FFW], weights[1])
            grad = grad + dot_t(full[half, rows, 2 * FFW :], weights[2])
            parts += [grad, dot_t(full[half, rows, :FFW], weights[0])]
        out_ref[rows] = jnp.concatenate(parts, axis=1).astype(BF)


def mix_kernel(pick_ref, gate_ref, back_ref, grad_ref, mixed_ref):
    totals = []
    for half in range(2):
        skip = half * (PAIR - JOIN)
        back = back_ref[:, half * JOIN : half * JOIN + STACK].astype(F32)
        lane = iota((1, STACK), 1)
        scaled = back * jnp.where(lane < skip + WIDE, 1.0, gate_ref[half])
        high = scaled.astype(BF)
        low = (scaled - high.astype(F32)).astype(BF)
        totals.append(t_dot(pick_ref[half], high) + t_dot(pick_ref[half], low))
    total = totals[0][:, :PAIR] + totals[1][:, STACK - PAIR :]
    grad_ref[...] = total[:, :WIDE].astype(BF)
    mixed_ref[...] = total[:, WIDE:].astype(BF)


HBM_SPEC = pl.BlockSpec(memory_space=pltpu.HBM)
VMEM_SPEC = pl.BlockSpec(memory_space=pltpu.VMEM)
SMEM_SPEC = pl.BlockSpec(memory_space=pltpu.SMEM)


def call(kernel, out_shape, *args, **kwargs):
    return pl.pallas_call(
        kernel,
        out_shape=out_shape,
        compiler_params=pltpu.CompilerParams(vmem_limit_bytes=VMEM_LIMIT),
        name=kernel.__name__,
        **kwargs,
    )(*args)


def in_hbm(*arrays):
    return [pltpu.with_memory_space_constraint(a, pltpu.HBM) for a in arrays]


def in_vmem(*arrays):
    return [pltpu.with_memory_space_constraint(a, pltpu.VMEM) for a in arrays]


def buffers(*arrays):
    return [pltpu.VMEM(a.shape, a.dtype) for a in arrays]


def semaphores(*counts):
    return [pltpu.SemaphoreType.DMA((n,)) for n in counts]


def to_experts(rows):
    rows = rows.reshape(EXPERTS, HALF, rows.shape[1])
    rows = lax.all_to_all(rows, "expert", split_axis=0, concat_axis=0, tiled=True)
    return rows.reshape(ROWS, -1)


def swap(array):
    return lax.ppermute(array, "core", [(0, 1), (1, 0)])


def after(array, *others):
    return lax.optimization_barrier((array,) + others)[0]


def body(tokens, expert_ids, gate_weights, w_gate, w_up, w_down, cotangent):
    gate_own, up_own, down_own = w_gate[0], w_up[0], w_down[0].T
    core = lax.axis_index("core")
    others = swap(jnp.concatenate([tokens, cotangent], axis=0))
    ids, gates = expert_ids.T, gate_weights.T
    inputs = (ids, gates, tokens, cotangent)
    send = call(
        send_kernel,
        shape(ROWS, 2 * PAIR),
        core.reshape(1),
        others,
        *in_hbm(*inputs),
        in_specs=[SMEM_SPEC, VMEM_SPEC] + [HBM_SPEC] * 4,
        scratch_shapes=buffers(*inputs) + semaphores(4),
    )
    rows = to_experts(send)
    gate_sent, up_sent, down_sent, _ = lax.optimization_barrier((gate_own, up_own, down_own, send))
    zeros = jnp.zeros((STACK - PAIR, FFW), BF)
    gate_stack = jnp.concatenate([gate_sent, swap(gate_sent), zeros], axis=0)
    up_stack = jnp.concatenate([up_sent, swap(up_sent), zeros], axis=0)
    down_stack = jnp.concatenate([zeros, down_sent, swap(down_sent)], axis=0)

    parts = call(
        sums_kernel,
        shape(ROWS, 3 * FFW),
        rows,
        *in_vmem(gate_stack, up_stack, down_stack),
        in_specs=[VMEM_SPEC] * 4,
        out_specs=HBM_SPEC,
        scratch_shapes=[pltpu.VMEM((ROWS, 3 * FFW), BF)] + semaphores(3),
    )
    sums = lax.psum_scatter(parts, "y", scatter_dimension=0, tiled=True)

    rows, ids, gates, _ = lax.optimization_barrier((rows, ids, gates, parts))
    pick, slot_gate = call(
        table_kernel,
        [shape(2, ROWS, tokens.shape[0]), shape(2, ROWS, 1, dtype=F32)],
        ids,
        gates,
    )
    own = jnp.concatenate([rows[:, :WIDE], rows[:, PAIR : PAIR + WIDE]], axis=1)
    other = jnp.concatenate([rows[:, WIDE:PAIR], rows[:, PAIR + WIDE :]], axis=1)
    other = swap(other)
    first = jnp.where(core == 0, own, other).reshape(N_Y, 1, SHARD, PAIR)
    second = jnp.where(core == 0, other, own).reshape(N_Y, 1, SHARD, PAIR)
    own = jnp.concatenate([first, second], axis=1).reshape(2 * ROWS, PAIR)
    rows_in, rows_dy = own[:, :WIDE], own[:, WIDE:]
    sums, rows_in, rows_dy, pick, slot_gate = lax.optimization_barrier(
        (sums, rows_in, rows_dy, pick, slot_gate)
    )

    shard = call(
        shard_kernel,
        shape(SHARD, 3 * FFW),
        *in_hbm(sums),
        in_specs=[HBM_SPEC],
        out_specs=HBM_SPEC,
        scratch_shapes=buffers(sums, sums) + semaphores(3, 3),
    )
    full = lax.all_gather(shard, ("y", "core"), axis=0, tiled=True)
    back = call(
        back_kernel,
        shape(ROWS, 2 * PAIR),
        *in_hbm(full, gate_own, up_own, down_own),
        in_specs=[HBM_SPEC] * 4,
        out_specs=VMEM_SPEC,
        scratch_shapes=[pltpu.VMEM((2, ROWS, 3 * FFW), BF), pltpu.VMEM((3, WIDE, FFW), BF)]
        + semaphores(3 + 2 * N_Y),
    )
    back = to_experts(back)

    grad_down = t_dot(rows_dy, full[:, :FFW]).astype(BF).T
    grad_gate = t_dot(rows_in, full[:, FFW : 2 * FFW]).astype(BF)
    grad_up = t_dot(rows_in, full[:, 2 * FFW :]).astype(BF)
    back = after(back, grad_down, grad_gate, grad_up)
    token_grad, mixed = call(mix_kernel, [shape(*tokens.shape)] * 2, pick, slot_gate, back)
    return mixed, token_grad, grad_gate[None], grad_up[None], grad_down[None]


def solution(mesh):
    fine = Mesh(mesh.devices.reshape(N_Y, 2, EXPERTS), ("y", "core", "expert"))
    dp = ("y", "core")
    placed = (
        P("expert", dp),
        P("expert", None),
        P("expert", None),
        P("expert", dp, None),
        P("expert", dp, None),
        P("expert", None, dp),
        P("expert", dp),
    )
    return jax.shard_map(
        body,
        mesh=fine,
        in_specs=placed,
        out_specs=(
            P("expert", dp),
            P("expert", dp),
            P("expert", dp, None),
            P("expert", dp, None),
            P("expert", None, dp),
        ),
        check_vma=False,
    )
```

```python
import jax
import jax.numpy as jnp
from jax import lax
from jax.experimental import pallas as pl
from jax.experimental.pallas import tpu as pltpu
from jax.sharding import Mesh, PartitionSpec as P

EXPERTS = 32
CAP = 32
HALF = CAP // 2
QUAD = 4
QUADS = HALF // QUAD
MAIN = QUADS - 1
QROWS = EXPERTS * QUAD
WIDE = 224
PAIR = 2 * WIDE
STACK = 512
JOIN = 2 * PAIR - STACK
FFW = 1024
N_Y = 8
BF = jnp.bfloat16
F32 = jnp.float32
VMEM_LIMIT = 24 * 1024 * 1024


def iota(shape, dim):
    return lax.broadcasted_iota(jnp.int32, shape, dim)


def dot(left, right):
    return jnp.dot(left, right, preferred_element_type=F32)


def dot_t(left, right):
    return lax.dot_general(left, right, (((1,), (1,)), ((), ())), preferred_element_type=F32)


def t_dot(left, right):
    return lax.dot_general(left, right, (((0,), (0,)), ((), ())), preferred_element_type=F32)


def shape(*dims, dtype=BF):
    return jax.ShapeDtypeStruct(dims, dtype)


def start(copies):
    for copy in copies:
        copy.start()


def wait(copies):
    for copy in copies:
        copy.wait()


def copies_of(pairs, sems):
    return [pltpu.make_async_copy(src, dst, sems.at[i]) for i, (src, dst) in enumerate(pairs)]


def slot_table(ids_ref, gates_ref, firsts):
    tokens = ids_ref.shape[1]
    numbers = iota((EXPERTS, tokens), 0)
    chosen = jnp.zeros((EXPERTS, tokens), F32)
    weight = jnp.zeros((EXPERTS, tokens), F32)
    for k in range(ids_ref.shape[0]):
        hit = ids_ref[k : k + 1, :] == numbers
        chosen = chosen + jnp.where(hit, 1.0, 0.0)
        weight = weight + jnp.where(hit, gates_ref[k : k + 1, :], 0.0)
    earlier = jnp.where(iota((tokens, tokens), 0) < iota((tokens, tokens), 1), 1.0, 0.0)
    rank = dot(chosen.astype(BF), earlier.astype(BF))
    rank = jnp.where(chosen > 0.5, rank, -1.0).astype(jnp.int32)
    tables = []
    for first in firsts:
        hit = (rank - first)[:, None, :] == iota((EXPERTS, QUAD, tokens), 1)
        pick = jnp.where(hit, 1.0, 0.0).reshape(QROWS, tokens)
        gate = jnp.where(hit, weight[:, None, :], 0.0).reshape(QROWS, tokens)
        tables.append((pick.astype(BF), jnp.sum(gate, axis=1, keepdims=True)))
    return tables


def send_kernel(
    core_ref,
    others_ref,
    ids_hbm,
    gates_hbm,
    tokens_hbm,
    cotangent_hbm,
    main_ref,
    last_ref,
    ids_ref,
    gates_ref,
    tokens_ref,
    cotangent_ref,
    sems,
):
    loads = copies_of(
        (
            (ids_hbm, ids_ref),
            (gates_hbm, gates_ref),
            (tokens_hbm, tokens_ref),
            (cotangent_hbm, cotangent_ref),
        ),
        sems,
    )
    start(loads)
    wait(loads[:2])
    firsts = [core_ref[0] * HALF + QUAD * q for q in range(QUADS)]
    tables = slot_table(ids_ref, gates_ref, firsts)
    wait(loads[2:])
    count = tokens_ref.shape[0]
    features = jnp.concatenate(
        [tokens_ref[...], others_ref[:count], cotangent_ref[...], others_ref[count:]], axis=1
    )
    for q, (pick, gate) in enumerate(tables):
        scale = jnp.where(iota((1, 2 * PAIR), 1) < PAIR, 1.0, gate)
        rows = (dot(pick, features) * scale).reshape(EXPERTS, QUAD, 2 * PAIR).astype(BF)
        if q < MAIN:
            main_ref[:, q] = rows
        else:
            last_ref[:, 0] = rows


def table_kernel(ids_ref, gates_ref, pick_ref, gate_ref):
    firsts = [QUAD * q for q in range(2 * QUADS)]
    for i, (pick, gate) in enumerate(slot_table(ids_ref, gates_ref, firsts)):
        half, q = i // QUADS, i % QUADS
        pick_ref[half, q * QROWS : (q + 1) * QROWS] = pick
        gate_ref[half, q * QROWS : (q + 1) * QROWS] = gate


def sums_kernel(quads, gate, up, down, rows, out_hbm, out, sems):
    columns = [pl.ds(i * FFW, FFW) for i in range(3)]
    stores = copies_of([(out.at[:, c], out_hbm.at[:, c]) for c in columns], sems)
    for q in range(quads.shape[1]):
        block = quads[:, q].astype(F32).reshape(QROWS, 2 * PAIR)
        rows[q * QROWS : (q + 1) * QROWS] = block.astype(BF)
    for i, weights in enumerate((gate, up, down)):
        left = rows[:, :STACK] if i < 2 else rows[:, 2 * PAIR - STACK :]
        out[:, i * FFW : (i + 1) * FFW] = dot(left, weights[...]).astype(BF)
        stores[i].start()
    wait(stores)


def hidden_arrays(gate_sum, up_sum, total):
    logistic = jax.nn.sigmoid(gate_sum)
    silu = gate_sum * logistic
    slope = logistic * (1.0 + gate_sum * (1.0 - logistic))
    return silu * up_sum, total * up_sum * slope, total * silu


def shard_kernel(sums_hbm, out_hbm, sums, out, in_sem, out_sem):
    load = pltpu.make_async_copy(sums_hbm, sums, in_sem.at[0])
    store = pltpu.make_async_copy(out, out_hbm, out_sem.at[0])
    load.start()
    load.wait()
    results = hidden_arrays(*[sums[:, i * FFW : (i + 1) * FFW].astype(F32) for i in range(3)])
    for i, result in enumerate(results):
        out[:, i * FFW : (i + 1) * FFW] = result.astype(BF)
    store.start()
    store.wait()


def add_kernel(parts_ref, out_ref):
    totals = []
    for i in range(3):
        columns = slice(i * FFW, (i + 1) * FFW)
        total = parts_ref[0, :, columns].astype(F32)
        for y in range(1, N_Y):
            total = total + parts_ref[y, :, columns].astype(F32)
        totals.append(total)
    for i, result in enumerate(hidden_arrays(*totals)):
        out_ref[:, i * FFW : (i + 1) * FFW] = result.astype(BF)


def back_parts(full, weights):
    grad = dot_t(full[:, FFW : 2 * FFW], weights[1]) + dot_t(full[:, 2 * FFW :], weights[2])
    return [grad, dot_t(full[:, :FFW], weights[0])]


def back_kernel(full_hbm, gate_hbm, up_hbm, down_hbm, out_ref, full, weights, sems):
    size = full.shape[1] // N_Y
    loads = copies_of(
        [(w, weights.at[i]) for i, w in enumerate((down_hbm, gate_hbm, up_hbm))]
        + [
            (full_hbm.at[pl.ds((2 * y + half) * size, size)], full.at[half, pl.ds(y * size, size)])
            for half in range(2)
            for y in range(N_Y)
        ],
        sems,
    )
    start(loads)
    wait(loads[:3])
    parts = []
    for half in range(2):
        wait(loads[3 + half * N_Y : 3 + (half + 1) * N_Y])
        parts += back_parts(full.at[half], weights)
    result = jnp.concatenate(parts, axis=1)
    for q in range(MAIN):
        block = result[q * QROWS : (q + 1) * QROWS]
        out_ref[:, q] = block.reshape(EXPERTS, QUAD, 2 * PAIR).astype(BF)


def back_last_kernel(core_ref, own, other, gate, up, down, out_ref):
    weights = (down[...], gate[...], up[...])
    own, other = back_parts(own, weights), back_parts(other, weights)
    is_first = core_ref[0] == 0
    result = jnp.where(
        is_first, jnp.concatenate(own + other, axis=1), jnp.concatenate(other + own, axis=1)
    )
    out_ref[:, 0] = result.reshape(EXPERTS, QUAD, 2 * PAIR).astype(BF)


def mix_kernel(pick_ref, gate_ref, main_ref, last_ref, grad_ref, mixed_ref):
    quads = [main_ref[:, q] for q in range(MAIN)] + [last_ref[:, 0]]
    back = jnp.concatenate([q.astype(F32).reshape(QROWS, 2 * PAIR) for q in quads], axis=0)
    totals = []
    for half in range(2):
        skip = half * (PAIR - JOIN)
        lane = iota((1, STACK), 1)
        scale = jnp.where(lane < skip + WIDE, 1.0, gate_ref[half])
        scaled = back[:, half * JOIN : half * JOIN + STACK] * scale
        high = scaled.astype(BF)
        low = (scaled - high.astype(F32)).astype(BF)
        totals.append(t_dot(pick_ref[half], high) + t_dot(pick_ref[half], low))
    total = totals[0][:, :PAIR] + totals[1][:, STACK - PAIR :]
    grad_ref[...] = total[:, :WIDE].astype(BF)
    mixed_ref[...] = total[:, WIDE:].astype(BF)


HBM_SPEC = pl.BlockSpec(memory_space=pltpu.HBM)
VMEM_SPEC = pl.BlockSpec(memory_space=pltpu.VMEM)
SMEM_SPEC = pl.BlockSpec(memory_space=pltpu.SMEM)


def call(kernel, out_shape, *args, **kwargs):
    return pl.pallas_call(
        kernel,
        out_shape=out_shape,
        compiler_params=pltpu.CompilerParams(vmem_limit_bytes=VMEM_LIMIT),
        name=kernel.__name__,
        **kwargs,
    )(*args)


def in_hbm(*arrays):
    return [pltpu.with_memory_space_constraint(a, pltpu.HBM) for a in arrays]


def in_vmem(*arrays):
    return [pltpu.with_memory_space_constraint(a, pltpu.VMEM) for a in arrays]


def buffers(*arrays):
    return [pltpu.VMEM(a.shape, a.dtype) for a in arrays]


def semaphores(*counts):
    return [pltpu.SemaphoreType.DMA((n,)) for n in counts]


def across(quads, axis):
    return lax.all_to_all(quads, axis, split_axis=0, concat_axis=0, tiled=True)


def swap(array):
    return lax.ppermute(array, "core", [(0, 1), (1, 0)])


def after(array, *others):
    return lax.optimization_barrier((array,) + others)[0]


def sums_call(quads, stacks):
    rows = quads.shape[1] * QROWS
    return call(
        sums_kernel,
        [shape(rows, 2 * PAIR), shape(rows, 3 * FFW)],
        quads,
        *in_vmem(*stacks),
        in_specs=[VMEM_SPEC] * 4,
        out_specs=[VMEM_SPEC, HBM_SPEC],
        scratch_shapes=[pltpu.VMEM((rows, 3 * FFW), BF)] + semaphores(3),
    )


def split_features(rows):
    own = jnp.concatenate([rows[:, :WIDE], rows[:, PAIR : PAIR + WIDE]], axis=1)
    other = jnp.concatenate([rows[:, WIDE:PAIR], rows[:, PAIR + WIDE :]], axis=1)
    return own, other


def grad_products(rows, full):
    rows_in, rows_dy = rows[:, :WIDE], rows[:, WIDE:]
    return (
        t_dot(rows_in, full[:, FFW : 2 * FFW]),
        t_dot(rows_in, full[:, 2 * FFW :]),
        t_dot(rows_dy, full[:, :FFW]),
    )


def body(tokens, expert_ids, gate_weights, w_gate, w_up, w_down, cotangent):
    gate_own, up_own, down_own = w_gate[0], w_up[0], w_down[0].T
    core = lax.axis_index("core")
    others = swap(jnp.concatenate([tokens, cotangent], axis=0))
    ids, gates = expert_ids.T, gate_weights.T
    inputs = (ids, gates, tokens, cotangent)
    send_main, send_last = call(
        send_kernel,
        [shape(EXPERTS, MAIN, QUAD, 2 * PAIR), shape(EXPERTS, 1, QUAD, 2 * PAIR)],
        core.reshape(1),
        others,
        *in_hbm(*inputs),
        in_specs=[SMEM_SPEC, VMEM_SPEC] + [HBM_SPEC] * 4,
        scratch_shapes=buffers(*inputs) + semaphores(4),
    )
    quads = across(send_main, "expert")
    gate_sent, up_sent, down_sent, _ = lax.optimization_barrier(
        (gate_own, up_own, down_own, send_main)
    )
    zeros = jnp.zeros((STACK - PAIR, FFW), BF)
    stacks = (
        jnp.concatenate([gate_sent, swap(gate_sent), zeros], axis=0),
        jnp.concatenate([up_sent, swap(up_sent), zeros], axis=0),
        jnp.concatenate([zeros, down_sent, swap(down_sent)], axis=0),
    )
    rows, parts = sums_call(quads, stacks)
    sums = lax.psum_scatter(parts, "y", scatter_dimension=0, tiled=True)

    quads = across(after(send_last, parts), "expert")
    rows_last, parts_last = sums_call(quads, stacks)
    parts_last = across(parts_last.reshape(N_Y, QROWS // N_Y, 3 * FFW), "y")

    sums = after(sums, parts_last)
    shard = call(
        shard_kernel,
        shape(*sums.shape),
        *in_hbm(sums),
        in_specs=[HBM_SPEC],
        out_specs=HBM_SPEC,
        scratch_shapes=buffers(sums, sums) + semaphores(1, 1),
    )
    full = lax.all_gather(shard, ("y", "core"), axis=0, tiled=True)

    shard_last = call(add_kernel, shape(QROWS // N_Y, 3 * FFW), after(parts_last, shard))
    full_last = lax.all_gather(shard_last, "y", axis=0, tiled=True)
    other_last = swap(full_last)
    back_last = call(
        back_last_kernel,
        shape(EXPERTS, 1, QUAD, 2 * PAIR),
        core.reshape(1),
        full_last,
        other_last,
        gate_own,
        up_own,
        down_own,
        in_specs=[SMEM_SPEC] + [VMEM_SPEC] * 5,
    )
    back_last = across(back_last, "expert")

    rows, rows_last, ids, gates, _ = lax.optimization_barrier(
        (rows, rows_last, ids, gates, shard_last)
    )
    pick, slot_gate = call(
        table_kernel,
        [
            shape(2, QUADS * QROWS, tokens.shape[0]),
            shape(2, QUADS * QROWS, 1, dtype=F32),
        ],
        ids,
        gates,
    )
    own, other = split_features(jnp.concatenate([rows, rows_last], axis=0))
    other = swap(other)
    count = MAIN * QROWS
    grads_last = [
        a + b
        for a, b in zip(
            grad_products(own[count:], full_last), grad_products(other[count:], other_last)
        )
    ]
    own, other = own[:count], other[:count]
    first = jnp.where(core == 0, own, other).reshape(N_Y, 1, -1, PAIR)
    second = jnp.where(core == 0, other, own).reshape(N_Y, 1, -1, PAIR)
    own = jnp.concatenate([first, second], axis=1).reshape(2 * count, PAIR)

    full, back_last, own, *grads_last = lax.optimization_barrier(
        (full, back_last, own, *grads_last)
    )
    back = call(
        back_kernel,
        shape(EXPERTS, MAIN, QUAD, 2 * PAIR),
        *in_hbm(full, gate_own, up_own, down_own),
        in_specs=[HBM_SPEC] * 4,
        out_specs=VMEM_SPEC,
        scratch_shapes=[pltpu.VMEM((2, count, 3 * FFW), BF), pltpu.VMEM((3, WIDE, FFW), BF)]
        + semaphores(3 + 2 * N_Y),
    )
    back = across(back, "expert")
    grads = [(a + b).astype(BF) for a, b in zip(grad_products(own, full), grads_last)]
    back = after(back, *grads)
    token_grad, mixed = call(
        mix_kernel, [shape(*tokens.shape)] * 2, pick, slot_gate, back, back_last
    )
    return mixed, token_grad, grads[0][None], grads[1][None], grads[2].T[None]


def solution(mesh):
    fine = Mesh(mesh.devices.reshape(N_Y, 2, EXPERTS), ("y", "core", "expert"))
    dp = ("y", "core")
    placed = (
        P("expert", dp),
        P("expert", None),
        P("expert", None),
        P("expert", dp, None),
        P("expert", dp, None),
        P("expert", None, dp),
        P("expert", dp),
    )
    return jax.shard_map(
        body,
        mesh=fine,
        in_specs=placed,
        out_specs=(
            P("expert", dp),
            P("expert", dp),
            P("expert", dp, None),
            P("expert", dp, None),
            P("expert", None, dp),
        ),
        check_vma=False,
    )
```

```python
import jax
import jax.numpy as jnp
from jax import lax
from jax.experimental import pallas as pl
from jax.experimental.pallas import tpu as pltpu
from jax.sharding import Mesh, PartitionSpec as P

EXPERTS = 32
CAP = 32
HALF = CAP // 2
QUAD = 4
QUADS = HALF // QUAD
MAIN = QUADS - 1
QROWS = EXPERTS * QUAD
ROWS = QUADS * QROWS
WIDE = 224
PAIR = 2 * WIDE
STACK = 512
JOIN = 2 * PAIR - STACK
FFW = 1024
N_Y = 8
PIECE = QROWS // N_Y
SHARD = ROWS // N_Y
BF = jnp.bfloat16
F32 = jnp.float32
VMEM_LIMIT = 24 * 1024 * 1024


def iota(shape, dim):
    return lax.broadcasted_iota(jnp.int32, shape, dim)


def dot(left, right):
    return jnp.dot(left, right, preferred_element_type=F32)


def dot_t(left, right):
    return lax.dot_general(left, right, (((1,), (1,)), ((), ())), preferred_element_type=F32)


def t_dot(left, right):
    return lax.dot_general(left, right, (((0,), (0,)), ((), ())), preferred_element_type=F32)


def shape(*dims, dtype=BF):
    return jax.ShapeDtypeStruct(dims, dtype)


def start(copies):
    for copy in copies:
        copy.start()


def wait(copies):
    for copy in copies:
        copy.wait()


def copies_of(pairs, sems):
    return [pltpu.make_async_copy(src, dst, sems.at[i]) for i, (src, dst) in enumerate(pairs)]


def slot_table(ids_ref, gates_ref, firsts):
    tokens = ids_ref.shape[1]
    numbers = iota((EXPERTS, tokens), 0)
    chosen = jnp.zeros((EXPERTS, tokens), F32)
    weight = jnp.zeros((EXPERTS, tokens), F32)
    for k in range(ids_ref.shape[0]):
        hit = ids_ref[k : k + 1, :] == numbers
        chosen = chosen + jnp.where(hit, 1.0, 0.0)
        weight = weight + jnp.where(hit, gates_ref[k : k + 1, :], 0.0)
    earlier = jnp.where(iota((tokens, tokens), 0) < iota((tokens, tokens), 1), 1.0, 0.0)
    rank = dot(chosen.astype(BF), earlier.astype(BF))
    rank = jnp.where(chosen > 0.5, rank, -1.0).astype(jnp.int32)
    tables = []
    for first in firsts:
        hit = (rank - first)[:, None, :] == iota((EXPERTS, QUAD, tokens), 1)
        pick = jnp.where(hit, 1.0, 0.0).reshape(QROWS, tokens)
        gate = jnp.where(hit, weight[:, None, :], 0.0).reshape(QROWS, tokens)
        tables.append((pick.astype(BF), jnp.sum(gate, axis=1, keepdims=True)))
    return tables


def send_kernel(
    core_ref,
    others_ref,
    ids_hbm,
    gates_hbm,
    tokens_hbm,
    cotangent_hbm,
    out_ref,
    ids_ref,
    gates_ref,
    tokens_ref,
    cotangent_ref,
    sems,
):
    loads = copies_of(
        (
            (ids_hbm, ids_ref),
            (gates_hbm, gates_ref),
            (tokens_hbm, tokens_ref),
            (cotangent_hbm, cotangent_ref),
        ),
        sems,
    )
    start(loads)
    wait(loads[:2])
    firsts = [core_ref[0] * HALF + QUAD * q for q in range(QUADS)]
    tables = slot_table(ids_ref, gates_ref, firsts)
    wait(loads[2:])
    count = tokens_ref.shape[0]
    features = jnp.concatenate(
        [tokens_ref[...], others_ref[:count], cotangent_ref[...], others_ref[count:]], axis=1
    )
    for q, (pick, gate) in enumerate(tables):
        scale = jnp.where(iota((1, 2 * PAIR), 1) < PAIR, 1.0, gate)
        rows = (dot(pick, features) * scale).reshape(EXPERTS, QUAD, 2 * PAIR)
        out_ref[:, q] = rows.astype(BF)


def table_kernel(ids_ref, gates_ref, pick_ref, gate_ref):
    firsts = [QUAD * q for q in range(2 * QUADS)]
    for i, (pick, gate) in enumerate(slot_table(ids_ref, gates_ref, firsts)):
        half, q = i // QUADS, i % QUADS
        pick_ref[half, q * QROWS : (q + 1) * QROWS] = pick
        gate_ref[half, q * QROWS : (q + 1) * QROWS] = gate


def sums_kernel(quads, gate, up, down, rows, out_hbm, out, sems):
    columns = [pl.ds(i * FFW, FFW) for i in range(3)]
    stores = copies_of([(out.at[:, c], out_hbm.at[:, c]) for c in columns], sems)
    for q in range(QUADS):
        block = quads[:, q].astype(F32).reshape(QROWS, 2 * PAIR).astype(BF)
        for y in range(N_Y):
            at = y * SHARD + q * PIECE
            rows[at : at + PIECE] = block[y * PIECE : (y + 1) * PIECE]
    for i, weights in enumerate((gate, up, down)):
        left = rows[:, :STACK] if i < 2 else rows[:, 2 * PAIR - STACK :]
        out[:, i * FFW : (i + 1) * FFW] = dot(left, weights[...]).astype(BF)
        stores[i].start()
    wait(stores)


def shard_kernel(sums_hbm, main_hbm, last_hbm, sums, out, in_sem, out_sems):
    load = pltpu.make_async_copy(sums_hbm, sums, in_sem.at[0])
    cut = SHARD - PIECE
    stores = copies_of(
        ((out.at[pl.ds(0, cut)], main_hbm), (out.at[pl.ds(cut, PIECE)], last_hbm)), out_sems
    )
    load.start()
    load.wait()
    gate_sum, up_sum, total = [sums[:, i * FFW : (i + 1) * FFW].astype(F32) for i in range(3)]
    logistic = jax.nn.sigmoid(gate_sum)
    silu = gate_sum * logistic
    slope = logistic * (1.0 + gate_sum * (1.0 - logistic))
    out[:, :FFW] = (silu * up_sum).astype(BF)
    out[:, FFW : 2 * FFW] = (total * up_sum * slope).astype(BF)
    out[:, 2 * FFW :] = (total * silu).astype(BF)
    start(stores)
    wait(stores)


def back_parts(full, weights):
    grad = dot_t(full[:, FFW : 2 * FFW], weights[1]) + dot_t(full[:, 2 * FFW :], weights[2])
    return [grad, dot_t(full[:, :FFW], weights[0])]


def back_kernel(full_hbm, gate_hbm, up_hbm, down_hbm, out_ref, full, weights, sems):
    size = full.shape[1] // N_Y
    loads = copies_of(
        [(w, weights.at[i]) for i, w in enumerate((down_hbm, gate_hbm, up_hbm))]
        + [
            (full_hbm.at[pl.ds((2 * y + half) * size, size)], full.at[half, pl.ds(y * size, size)])
            for half in range(2)
            for y in range(N_Y)
        ],
        sems,
    )
    start(loads)
    wait(loads[:3])
    parts = []
    for half in range(2):
        wait(loads[3 + half * N_Y : 3 + (half + 1) * N_Y])
        parts += back_parts(full.at[half], weights)
    result = jnp.concatenate(parts, axis=1)
    for q in range(MAIN):
        starts = [y * size + q * PIECE for y in range(N_Y)]
        block = jnp.concatenate([result[at : at + PIECE] for at in starts], axis=0)
        out_ref[:, q] = block.reshape(EXPERTS, QUAD, 2 * PAIR).astype(BF)


def back_last_kernel(full, gate, up, down, out_ref):
    result = dot_t(full[:, :FFW], down[...])
    grad = dot_t(full[:, FFW : 2 * FFW], gate[...]) + dot_t(full[:, 2 * FFW :], up[...])
    middle = grad[:, JOIN:] + result[:, : STACK - JOIN]
    rows = jnp.concatenate([grad[:, :JOIN], middle, result[:, STACK - JOIN :]], axis=1)
    out_ref[:, 0] = rows.reshape(EXPERTS, QUAD, 2 * PAIR).astype(BF)


def gated_sum(pick, scaled):
    high = scaled.astype(BF)
    low = (scaled - high.astype(F32)).astype(BF)
    return t_dot(pick, high) + t_dot(pick, low)


def mix_last_kernel(core_ref, pick_ref, gate_ref, last_ref, out_ref):
    back = last_ref[:, 0].astype(F32).reshape(QROWS, 2 * PAIR)
    rows = pl.ds(MAIN * QROWS, QROWS)
    scale = jnp.where(iota((1, 2 * PAIR), 1) < PAIR, 1.0, gate_ref[core_ref[0], rows])
    out_ref[...] = gated_sum(pick_ref[core_ref[0], rows], back * scale)


def mix_kernel(pick_ref, gate_ref, main_ref, own_ref, other_ref, grad_ref, mixed_ref):
    quads = [main_ref[:, q] for q in range(MAIN)]
    back = jnp.concatenate([q.astype(F32).reshape(QROWS, 2 * PAIR) for q in quads], axis=0)
    rows = slice(0, MAIN * QROWS)
    totals = []
    for half in range(2):
        skip = half * (PAIR - JOIN)
        lane = iota((1, STACK), 1)
        scale = jnp.where(lane < skip + WIDE, 1.0, gate_ref[half, rows])
        scaled = back[:, half * JOIN : half * JOIN + STACK] * scale
        totals.append(gated_sum(pick_ref[half, rows], scaled))
    total = totals[0][:, :PAIR] + totals[1][:, STACK - PAIR :]
    own, other = own_ref[...], other_ref[...]
    grad = total[:, :WIDE] + own[:, :WIDE] + other[:, WIDE:PAIR]
    mixed = total[:, WIDE:] + own[:, PAIR : PAIR + WIDE] + other[:, PAIR + WIDE :]
    grad_ref[...] = grad.astype(BF)
    mixed_ref[...] = mixed.astype(BF)


HBM_SPEC = pl.BlockSpec(memory_space=pltpu.HBM)
VMEM_SPEC = pl.BlockSpec(memory_space=pltpu.VMEM)
SMEM_SPEC = pl.BlockSpec(memory_space=pltpu.SMEM)


def call(kernel, out_shape, *args, **kwargs):
    return pl.pallas_call(
        kernel,
        out_shape=out_shape,
        compiler_params=pltpu.CompilerParams(vmem_limit_bytes=VMEM_LIMIT),
        name=kernel.__name__,
        **kwargs,
    )(*args)


def in_hbm(*arrays):
    return [pltpu.with_memory_space_constraint(a, pltpu.HBM) for a in arrays]


def in_vmem(*arrays):
    return [pltpu.with_memory_space_constraint(a, pltpu.VMEM) for a in arrays]


def buffers(*arrays):
    return [pltpu.VMEM(a.shape, a.dtype) for a in arrays]


def semaphores(*counts):
    return [pltpu.SemaphoreType.DMA((n,)) for n in counts]


def across(quads, axis):
    return lax.all_to_all(quads, axis, split_axis=0, concat_axis=0, tiled=True)


def swap(array):
    return lax.ppermute(array, "core", [(0, 1), (1, 0)])


def after(array, *others):
    return lax.optimization_barrier((array,) + others)[0]


def split_features(rows):
    own = jnp.concatenate([rows[:, :WIDE], rows[:, PAIR : PAIR + WIDE]], axis=1)
    other = jnp.concatenate([rows[:, WIDE:PAIR], rows[:, PAIR + WIDE :]], axis=1)
    return own, other


def grad_products(rows, full):
    rows_in, rows_dy = rows[:, :WIDE], rows[:, WIDE:]
    return (
        t_dot(rows_in, full[:, FFW : 2 * FFW]),
        t_dot(rows_in, full[:, 2 * FFW :]),
        t_dot(rows_dy, full[:, :FFW]),
    )


def body(tokens, expert_ids, gate_weights, w_gate, w_up, w_down, cotangent):
    gate_own, up_own, down_own = w_gate[0], w_up[0], w_down[0].T
    core = lax.axis_index("core")
    others = swap(jnp.concatenate([tokens, cotangent], axis=0))
    ids, gates = expert_ids.T, gate_weights.T
    inputs = (ids, gates, tokens, cotangent)
    send = call(
        send_kernel,
        shape(EXPERTS, QUADS, QUAD, 2 * PAIR),
        core.reshape(1),
        others,
        *in_hbm(*inputs),
        in_specs=[SMEM_SPEC, VMEM_SPEC] + [HBM_SPEC] * 4,
        scratch_shapes=buffers(*inputs) + semaphores(4),
    )
    quads = across(send, "expert")
    gate_sent, up_sent, down_sent, _ = lax.optimization_barrier((gate_own, up_own, down_own, send))
    zeros = jnp.zeros((STACK - PAIR, FFW), BF)
    stacks = (
        jnp.concatenate([gate_sent, swap(gate_sent), zeros], axis=0),
        jnp.concatenate([up_sent, swap(up_sent), zeros], axis=0),
        jnp.concatenate([zeros, down_sent, swap(down_sent)], axis=0),
    )
    rows, parts = call(
        sums_kernel,
        [shape(ROWS, 2 * PAIR), shape(ROWS, 3 * FFW)],
        quads,
        *in_vmem(*stacks),
        in_specs=[VMEM_SPEC] * 4,
        out_specs=[VMEM_SPEC, HBM_SPEC],
        scratch_shapes=[pltpu.VMEM((ROWS, 3 * FFW), BF)] + semaphores(3),
    )
    sums = lax.psum_scatter(parts, "y", scatter_dimension=0, tiled=True)

    rows, ids, gates, _ = lax.optimization_barrier((rows, ids, gates, parts))
    pick, slot_gate = call(
        table_kernel,
        [shape(2, ROWS, tokens.shape[0]), shape(2, ROWS, 1, dtype=F32)],
        ids,
        gates,
    )
    own, other = split_features(rows)
    other = swap(other)
    own, other = own.reshape(N_Y, SHARD, PAIR), other.reshape(N_Y, SHARD, PAIR)
    cut = SHARD - PIECE
    own_last = own[:, cut:].reshape(QROWS, PAIR)
    other_last = other[:, cut:].reshape(QROWS, PAIR)
    first = jnp.where(core == 0, own, other)[:, None, :cut]
    second = jnp.where(core == 0, other, own)[:, None, :cut]
    main = jnp.concatenate([first, second], axis=1).reshape(2 * MAIN * QROWS, PAIR)
    sums, main, own_last, other_last, pick, slot_gate = lax.optimization_barrier(
        (sums, main, own_last, other_last, pick, slot_gate)
    )

    shard, shard_last = call(
        shard_kernel,
        [shape(cut, 3 * FFW), shape(PIECE, 3 * FFW)],
        *in_hbm(sums),
        in_specs=[HBM_SPEC],
        out_specs=[HBM_SPEC] * 2,
        scratch_shapes=buffers(sums, sums) + semaphores(1, 2),
    )
    full = lax.all_gather(shard, ("y", "core"), axis=0, tiled=True)

    full_last = lax.all_gather(shard_last, "y", axis=0, tiled=True)
    send_last = call(
        back_last_kernel, shape(EXPERTS, 1, QUAD, 2 * PAIR), full_last, *in_vmem(*stacks)
    )
    back_last = across(send_last, "expert")
    full_last = after(full_last, send_last)
    grads_last = [
        a + b
        for a, b in zip(
            grad_products(own_last, full_last), grad_products(other_last, swap(full_last))
        )
    ]

    back = call(
        back_kernel,
        shape(EXPERTS, MAIN, QUAD, 2 * PAIR),
        *in_hbm(full, gate_own, up_own, down_own),
        in_specs=[HBM_SPEC] * 4,
        out_specs=VMEM_SPEC,
        scratch_shapes=[
            pltpu.VMEM((2, MAIN * QROWS, 3 * FFW), BF),
            pltpu.VMEM((3, WIDE, FFW), BF),
        ]
        + semaphores(3 + 2 * N_Y),
    )
    back_last = after(back_last, back)
    total_last = call(
        mix_last_kernel,
        shape(tokens.shape[0], 2 * PAIR, dtype=F32),
        core.reshape(1),
        pick,
        slot_gate,
        back_last,
        in_specs=[SMEM_SPEC] + [VMEM_SPEC] * 3,
    )
    other_total = swap(total_last)
    back = across(back, "expert")
    grads = [(a + b).astype(BF) for a, b in zip(grad_products(main, full), grads_last)]
    back = after(back, other_total, *grads)
    token_grad, mixed = call(
        mix_kernel, [shape(*tokens.shape)] * 2, pick, slot_gate, back, total_last, other_total
    )
    return mixed, token_grad, grads[0][None], grads[1][None], grads[2].T[None]


def solution(mesh):
    fine = Mesh(mesh.devices.reshape(N_Y, 2, EXPERTS), ("y", "core", "expert"))
    dp = ("y", "core")
    placed = (
        P("expert", dp),
        P("expert", None),
        P("expert", None),
        P("expert", dp, None),
        P("expert", dp, None),
        P("expert", None, dp),
        P("expert", dp),
    )
    return jax.shard_map(
        body,
        mesh=fine,
        in_specs=placed,
        out_specs=(
            P("expert", dp),
            P("expert", dp),
            P("expert", dp, None),
            P("expert", dp, None),
            P("expert", None, dp),
        ),
        check_vma=False,
    )
```

```python
import jax
import jax.numpy as jnp
from jax import lax
from jax.experimental import pallas as pl
from jax.experimental.pallas import tpu as pltpu
from jax.sharding import Mesh, PartitionSpec as P

EXPERTS = 32
CAP = 32
HALF = CAP // 2
QUAD = 4
QUADS = HALF // QUAD
MAIN = QUADS - 1
QROWS = EXPERTS * QUAD
ROWS = QUADS * QROWS
WIDE = 224
PAIR = 2 * WIDE
STACK = 512
JOIN = 2 * PAIR - STACK
FFW = 1024
N_Y = 8
PIECE = QROWS // N_Y
SHARD = ROWS // N_Y
BF = jnp.bfloat16
F32 = jnp.float32
VMEM_LIMIT = 24 * 1024 * 1024


def iota(shape, dim):
    return lax.broadcasted_iota(jnp.int32, shape, dim)


def dot(left, right):
    return jnp.dot(left, right, preferred_element_type=F32)


def dot_t(left, right):
    return lax.dot_general(left, right, (((1,), (1,)), ((), ())), preferred_element_type=F32)


def t_dot(left, right):
    return lax.dot_general(left, right, (((0,), (0,)), ((), ())), preferred_element_type=F32)


def shape(*dims, dtype=BF):
    return jax.ShapeDtypeStruct(dims, dtype)


def start(copies):
    for copy in copies:
        copy.start()


def wait(copies):
    for copy in copies:
        copy.wait()


def copies_of(pairs, sems):
    return [pltpu.make_async_copy(src, dst, sems.at[i]) for i, (src, dst) in enumerate(pairs)]


def slot_table(ids_ref, gates_ref, firsts):
    tokens = ids_ref.shape[1]
    numbers = iota((EXPERTS, tokens), 0)
    chosen = jnp.zeros((EXPERTS, tokens), F32)
    weight = jnp.zeros((EXPERTS, tokens), F32)
    for k in range(ids_ref.shape[0]):
        hit = ids_ref[k : k + 1, :] == numbers
        chosen = chosen + jnp.where(hit, 1.0, 0.0)
        weight = weight + jnp.where(hit, gates_ref[k : k + 1, :], 0.0)
    earlier = jnp.where(iota((tokens, tokens), 0) < iota((tokens, tokens), 1), 1.0, 0.0)
    rank = dot(chosen.astype(BF), earlier.astype(BF))
    rank = jnp.where(chosen > 0.5, rank, -1.0).astype(jnp.int32)
    tables = []
    for first in firsts:
        hit = (rank - first)[:, None, :] == iota((EXPERTS, QUAD, tokens), 1)
        pick = jnp.where(hit, 1.0, 0.0).reshape(QROWS, tokens)
        gate = jnp.where(hit, weight[:, None, :], 0.0).reshape(QROWS, tokens)
        tables.append((pick.astype(BF), jnp.sum(gate, axis=1, keepdims=True)))
    return tables


def send_kernel(
    core_ref,
    others_ref,
    ids_hbm,
    gates_hbm,
    tokens_hbm,
    cotangent_hbm,
    out_ref,
    ids_ref,
    gates_ref,
    tokens_ref,
    cotangent_ref,
    sems,
):
    loads = copies_of(
        (
            (ids_hbm, ids_ref),
            (gates_hbm, gates_ref),
            (tokens_hbm, tokens_ref),
            (cotangent_hbm, cotangent_ref),
        ),
        sems,
    )
    start(loads)
    wait(loads[:2])
    firsts = [core_ref[0] * HALF + QUAD * q for q in range(QUADS)]
    tables = slot_table(ids_ref, gates_ref, firsts)
    wait(loads[2:])
    count = tokens_ref.shape[0]
    features = jnp.concatenate(
        [tokens_ref[...], others_ref[:count], cotangent_ref[...], others_ref[count:]], axis=1
    )
    for q, (pick, gate) in enumerate(tables):
        scale = jnp.where(iota((1, 2 * PAIR), 1) < PAIR, 1.0, gate)
        rows = (dot(pick, features) * scale).reshape(EXPERTS, QUAD, 2 * PAIR)
        out_ref[:, q] = rows.astype(BF)


def table_kernel(ids_ref, gates_ref, pick_ref, gate_ref):
    firsts = [QUAD * q for q in range(2 * QUADS)]
    for i, (pick, gate) in enumerate(slot_table(ids_ref, gates_ref, firsts)):
        half, q = i // QUADS, i % QUADS
        pick_ref[half, q * QROWS : (q + 1) * QROWS] = pick
        gate_ref[half, q * QROWS : (q + 1) * QROWS] = gate


def sums_kernel(quads, gate, up, down, rows_hbm, out_hbm, rows, out, sems):
    columns = [pl.ds(i * FFW, FFW) for i in range(3)]
    stores = copies_of([(out.at[:, c], out_hbm.at[:, c]) for c in columns], sems)
    for q in range(QUADS):
        block = quads[:, q].astype(F32).reshape(QROWS, 2 * PAIR).astype(BF)
        for y in range(N_Y):
            at = y * SHARD + q * PIECE
            rows[at : at + PIECE] = block[y * PIECE : (y + 1) * PIECE]
    rows_store = pltpu.make_async_copy(rows, rows_hbm, sems.at[3])
    rows_store.start()
    for i, weights in enumerate((gate, up, down)):
        left = rows[:, :STACK] if i < 2 else rows[:, 2 * PAIR - STACK :]
        out[:, i * FFW : (i + 1) * FFW] = dot(left, weights[...]).astype(BF)
        stores[i].start()
    wait(stores + [rows_store])


def shard_kernel(sums_hbm, main_hbm, last_ref, sums, main, in_sem, out_sem):
    load = pltpu.make_async_copy(sums_hbm, sums, in_sem.at[0])
    store = pltpu.make_async_copy(main, main_hbm, out_sem.at[0])
    load.start()
    load.wait()
    gate_sum, up_sum, total = [sums[:, i * FFW : (i + 1) * FFW].astype(F32) for i in range(3)]
    logistic = jax.nn.sigmoid(gate_sum)
    silu = gate_sum * logistic
    slope = logistic * (1.0 + gate_sum * (1.0 - logistic))
    results = [silu * up_sum, total * up_sum * slope, total * silu]
    cut = SHARD - PIECE
    for i, result in enumerate(results):
        main[:, i * FFW : (i + 1) * FFW] = result[:cut].astype(BF)
    store.start()
    for i, result in enumerate(results):
        last_ref[:, i * FFW : (i + 1) * FFW] = result[cut:].astype(BF)
    store.wait()


def back_parts(full, weights):
    grad = dot_t(full[:, FFW : 2 * FFW], weights[1]) + dot_t(full[:, 2 * FFW :], weights[2])
    return [grad, dot_t(full[:, :FFW], weights[0])]


def back_kernel(full_hbm, gate_hbm, up_hbm, down_hbm, out_ref, full, weights, sems):
    size = full.shape[1] // N_Y
    loads = copies_of(
        [(w, weights.at[i]) for i, w in enumerate((down_hbm, gate_hbm, up_hbm))]
        + [
            (full_hbm.at[pl.ds((2 * y + half) * size, size)], full.at[half, pl.ds(y * size, size)])
            for half in range(2)
            for y in range(N_Y)
        ],
        sems,
    )
    start(loads)
    wait(loads[:3])
    parts = []
    for half in range(2):
        wait(loads[3 + half * N_Y : 3 + (half + 1) * N_Y])
        parts += back_parts(full.at[half], weights)
    result = jnp.concatenate(parts, axis=1)
    for q in range(MAIN):
        starts = [y * size + q * PIECE for y in range(N_Y)]
        block = jnp.concatenate([result[at : at + PIECE] for at in starts], axis=0)
        out_ref[:, q] = block.reshape(EXPERTS, QUAD, 2 * PAIR).astype(BF)


def back_last_kernel(full, gate, up, down, out_ref):
    result = dot_t(full[:, :FFW], down[...])
    grad = dot_t(full[:, FFW : 2 * FFW], gate[...]) + dot_t(full[:, 2 * FFW :], up[...])
    middle = grad[:, JOIN:] + result[:, : STACK - JOIN]
    rows = jnp.concatenate([grad[:, :JOIN], middle, result[:, STACK - JOIN :]], axis=1)
    out_ref[:, 0] = rows.reshape(EXPERTS, QUAD, 2 * PAIR).astype(BF)


def gated_sum(pick, scaled):
    high = scaled.astype(BF)
    low = (scaled - high.astype(F32)).astype(BF)
    return t_dot(pick, high) + t_dot(pick, low)


def mix_last_kernel(core_ref, pick_ref, gate_ref, last_ref, out_ref):
    back = last_ref[:, 0].astype(F32).reshape(QROWS, 2 * PAIR)
    rows = pl.ds(MAIN * QROWS, QROWS)
    scale = jnp.where(iota((1, 2 * PAIR), 1) < PAIR, 1.0, gate_ref[core_ref[0], rows])
    out_ref[...] = gated_sum(pick_ref[core_ref[0], rows], back * scale)


def mix_kernel(pick_ref, gate_ref, main_ref, own_ref, other_ref, grad_ref, mixed_ref):
    quads = [main_ref[:, q] for q in range(MAIN)]
    back = jnp.concatenate([q.astype(F32).reshape(QROWS, 2 * PAIR) for q in quads], axis=0)
    rows = slice(0, MAIN * QROWS)
    totals = []
    for half in range(2):
        skip = half * (PAIR - JOIN)
        lane = iota((1, STACK), 1)
        scale = jnp.where(lane < skip + WIDE, 1.0, gate_ref[half, rows])
        scaled = back[:, half * JOIN : half * JOIN + STACK] * scale
        totals.append(gated_sum(pick_ref[half, rows], scaled))
    total = totals[0][:, :PAIR] + totals[1][:, STACK - PAIR :]
    own, other = own_ref[...], other_ref[...]
    grad = total[:, :WIDE] + own[:, :WIDE] + other[:, WIDE:PAIR]
    mixed = total[:, WIDE:] + own[:, PAIR : PAIR + WIDE] + other[:, PAIR + WIDE :]
    grad_ref[...] = grad.astype(BF)
    mixed_ref[...] = mixed.astype(BF)


HBM_SPEC = pl.BlockSpec(memory_space=pltpu.HBM)
VMEM_SPEC = pl.BlockSpec(memory_space=pltpu.VMEM)
SMEM_SPEC = pl.BlockSpec(memory_space=pltpu.SMEM)


def call(kernel, out_shape, *args, **kwargs):
    return pl.pallas_call(
        kernel,
        out_shape=out_shape,
        compiler_params=pltpu.CompilerParams(vmem_limit_bytes=VMEM_LIMIT),
        name=kernel.__name__,
        **kwargs,
    )(*args)


def in_hbm(*arrays):
    return [pltpu.with_memory_space_constraint(a, pltpu.HBM) for a in arrays]


def in_vmem(*arrays):
    return [pltpu.with_memory_space_constraint(a, pltpu.VMEM) for a in arrays]


def buffers(*arrays):
    return [pltpu.VMEM(a.shape, a.dtype) for a in arrays]


def semaphores(*counts):
    return [pltpu.SemaphoreType.DMA((n,)) for n in counts]


def across(quads, axis):
    return lax.all_to_all(quads, axis, split_axis=0, concat_axis=0, tiled=True)


def swap(array):
    return lax.ppermute(array, "core", [(0, 1), (1, 0)])


def after(array, *others):
    return lax.optimization_barrier((array,) + others)[0]


def split_features(rows):
    own = jnp.concatenate([rows[:, :WIDE], rows[:, PAIR : PAIR + WIDE]], axis=1)
    other = jnp.concatenate([rows[:, WIDE:PAIR], rows[:, PAIR + WIDE :]], axis=1)
    return own, other


def grad_products(rows, full):
    rows_in, rows_dy = rows[:, :WIDE], rows[:, WIDE:]
    return (
        t_dot(rows_in, full[:, FFW : 2 * FFW]),
        t_dot(rows_in, full[:, 2 * FFW :]),
        t_dot(rows_dy, full[:, :FFW]),
    )


def body(tokens, expert_ids, gate_weights, w_gate, w_up, w_down, cotangent):
    gate_own, up_own, down_own = w_gate[0], w_up[0], w_down[0].T
    core = lax.axis_index("core")
    others = swap(jnp.concatenate([tokens, cotangent], axis=0))
    ids, gates = expert_ids.T, gate_weights.T
    inputs = (ids, gates, tokens, cotangent)
    send = call(
        send_kernel,
        shape(EXPERTS, QUADS, QUAD, 2 * PAIR),
        core.reshape(1),
        others,
        *in_hbm(*inputs),
        in_specs=[SMEM_SPEC, VMEM_SPEC] + [HBM_SPEC] * 4,
        scratch_shapes=buffers(*inputs) + semaphores(4),
    )
    quads = across(send, "expert")
    gate_sent, up_sent, down_sent, _ = lax.optimization_barrier((gate_own, up_own, down_own, send))
    zeros = jnp.zeros((STACK - PAIR, FFW), BF)
    stacks = (
        jnp.concatenate([gate_sent, swap(gate_sent), zeros], axis=0),
        jnp.concatenate([up_sent, swap(up_sent), zeros], axis=0),
        jnp.concatenate([zeros, down_sent, swap(down_sent)], axis=0),
    )
    rows, parts = call(
        sums_kernel,
        [pltpu.HBM((ROWS, 2 * PAIR), BF), pltpu.HBM((ROWS, 3 * FFW), BF)],
        quads,
        *in_vmem(*stacks),
        in_specs=[VMEM_SPEC] * 4,
        out_specs=[HBM_SPEC] * 2,
        scratch_shapes=[pltpu.VMEM((ROWS, 2 * PAIR), BF), pltpu.VMEM((ROWS, 3 * FFW), BF)]
        + semaphores(4),
    )
    sums = lax.psum_scatter(parts, "y", scatter_dimension=0, tiled=True)

    rows, ids, gates, _ = lax.optimization_barrier((rows, ids, gates, parts))
    pick, slot_gate = call(
        table_kernel,
        [shape(2, ROWS, tokens.shape[0]), shape(2, ROWS, 1, dtype=F32)],
        ids,
        gates,
    )
    own, other = split_features(rows)
    other = swap(other)
    own, other = own.reshape(N_Y, SHARD, PAIR), other.reshape(N_Y, SHARD, PAIR)
    cut = SHARD - PIECE
    own_last = own[:, cut:].reshape(QROWS, PAIR)
    other_last = other[:, cut:].reshape(QROWS, PAIR)
    first = jnp.where(core == 0, own, other)[:, None, :cut]
    second = jnp.where(core == 0, other, own)[:, None, :cut]
    main = jnp.concatenate([first, second], axis=1).reshape(2 * MAIN * QROWS, PAIR)
    sums, main, own_last, other_last, pick, slot_gate = lax.optimization_barrier(
        (sums, main, own_last, other_last, pick, slot_gate)
    )

    shard_shape = shape(cut, 3 * FFW)
    shard, shard_last = call(
        shard_kernel,
        [pltpu.HBM((cut, 3 * FFW), BF), shape(PIECE, 3 * FFW)],
        *in_hbm(sums),
        in_specs=[HBM_SPEC],
        out_specs=[HBM_SPEC, VMEM_SPEC],
        scratch_shapes=buffers(sums, shard_shape) + semaphores(1, 1),
    )
    full = lax.all_gather(shard, ("y", "core"), axis=0, tiled=True)

    full_last = lax.all_gather(shard_last, "y", axis=0, tiled=True)
    send_last = call(
        back_last_kernel, shape(EXPERTS, 1, QUAD, 2 * PAIR), full_last, *in_vmem(*stacks)
    )
    back_last = across(send_last, "expert")

    back = call(
        back_kernel,
        shape(EXPERTS, MAIN, QUAD, 2 * PAIR),
        *in_hbm(full, gate_own, up_own, down_own),
        in_specs=[HBM_SPEC] * 4,
        out_specs=VMEM_SPEC,
        scratch_shapes=[
            pltpu.VMEM((2, MAIN * QROWS, 3 * FFW), BF),
            pltpu.VMEM((3, WIDE, FFW), BF),
        ]
        + semaphores(3 + 2 * N_Y),
    )
    back_last = after(back_last, back)
    total_last = call(
        mix_last_kernel,
        shape(tokens.shape[0], 2 * PAIR, dtype=F32),
        core.reshape(1),
        pick,
        slot_gate,
        back_last,
        in_specs=[SMEM_SPEC] + [VMEM_SPEC] * 3,
    )
    other_total = swap(total_last)
    back = across(back, "expert")
    full_last = after(full_last, total_last)
    grads_last = [
        a + b
        for a, b in zip(
            grad_products(own_last, full_last), grad_products(other_last, swap(full_last))
        )
    ]
    grads = [(a + b).astype(BF) for a, b in zip(grad_products(main, full), grads_last)]
    back = after(back, other_total, *grads)
    token_grad, mixed = call(
        mix_kernel, [shape(*tokens.shape)] * 2, pick, slot_gate, back, total_last, other_total
    )
    return mixed, token_grad, grads[0][None], grads[1][None], grads[2].T[None]


def solution(mesh):
    fine = Mesh(mesh.devices.reshape(N_Y, 2, EXPERTS), ("y", "core", "expert"))
    dp = ("y", "core")
    placed = (
        P("expert", dp),
        P("expert", None),
        P("expert", None),
        P("expert", dp, None),
        P("expert", dp, None),
        P("expert", None, dp),
        P("expert", dp),
    )
    return jax.shard_map(
        body,
        mesh=fine,
        in_specs=placed,
        out_specs=(
            P("expert", dp),
            P("expert", dp),
            P("expert", dp, None),
            P("expert", dp, None),
            P("expert", None, dp),
        ),
        check_vma=False,
    )
```

```python
import jax
import jax.numpy as jnp
from jax import lax
from jax.experimental import pallas as pl
from jax.experimental.pallas import tpu as pltpu
from jax.sharding import Mesh, PartitionSpec as P

EXPERTS = 32
CAP = 32
HALF = CAP // 2
QUAD = 4
QUADS = HALF // QUAD
MAIN = QUADS - 1
QROWS = EXPERTS * QUAD
ROWS = QUADS * QROWS
WIDE = 224
PAIR = 2 * WIDE
STACK = 512
JOIN = 2 * PAIR - STACK
FFW = 1024
N_Y = 8
PIECE = QROWS // N_Y
SHARD = ROWS // N_Y
BF = jnp.bfloat16
F32 = jnp.float32
VMEM_LIMIT = 24 * 1024 * 1024


def iota(shape, dim):
    return lax.broadcasted_iota(jnp.int32, shape, dim)


def dot(left, right):
    return jnp.dot(left, right, preferred_element_type=F32)


def dot_t(left, right):
    return lax.dot_general(left, right, (((1,), (1,)), ((), ())), preferred_element_type=F32)


def t_dot(left, right):
    return lax.dot_general(left, right, (((0,), (0,)), ((), ())), preferred_element_type=F32)


def shape(*dims, dtype=BF):
    return jax.ShapeDtypeStruct(dims, dtype)


def start(copies):
    for copy in copies:
        copy.start()


def wait(copies):
    for copy in copies:
        copy.wait()


def copies_of(pairs, sems):
    return [pltpu.make_async_copy(src, dst, sems.at[i]) for i, (src, dst) in enumerate(pairs)]


def slot_table(ids_ref, gates_ref, firsts):
    tokens = ids_ref.shape[1]
    numbers = iota((EXPERTS, tokens), 0)
    chosen = jnp.zeros((EXPERTS, tokens), F32)
    weight = jnp.zeros((EXPERTS, tokens), F32)
    for k in range(ids_ref.shape[0]):
        hit = ids_ref[k : k + 1, :] == numbers
        chosen = chosen + jnp.where(hit, 1.0, 0.0)
        weight = weight + jnp.where(hit, gates_ref[k : k + 1, :], 0.0)
    earlier = jnp.where(iota((tokens, tokens), 0) < iota((tokens, tokens), 1), 1.0, 0.0)
    rank = dot(chosen.astype(BF), earlier.astype(BF))
    rank = jnp.where(chosen > 0.5, rank, -1.0).astype(jnp.int32)
    tables = []
    for first in firsts:
        hit = (rank - first)[:, None, :] == iota((EXPERTS, QUAD, tokens), 1)
        pick = jnp.where(hit, 1.0, 0.0).reshape(QROWS, tokens)
        gate = jnp.where(hit, weight[:, None, :], 0.0).reshape(QROWS, tokens)
        tables.append((pick.astype(BF), jnp.sum(gate, axis=1, keepdims=True)))
    return tables


def send_kernel(
    core_ref,
    others_ref,
    ids_hbm,
    gates_hbm,
    tokens_hbm,
    cotangent_hbm,
    out_ref,
    ids_ref,
    gates_ref,
    tokens_ref,
    cotangent_ref,
    sems,
):
    loads = copies_of(
        (
            (ids_hbm, ids_ref),
            (gates_hbm, gates_ref),
            (tokens_hbm, tokens_ref),
            (cotangent_hbm, cotangent_ref),
        ),
        sems,
    )
    start(loads)
    wait(loads[:2])
    firsts = [core_ref[0] * HALF + QUAD * q for q in range(QUADS)]
    tables = slot_table(ids_ref, gates_ref, firsts)
    wait(loads[2:])
    count = tokens_ref.shape[0]
    features = jnp.concatenate(
        [tokens_ref[...], others_ref[:count], cotangent_ref[...], others_ref[count:]], axis=1
    )
    for q, (pick, gate) in enumerate(tables):
        scale = jnp.where(iota((1, 2 * PAIR), 1) < PAIR, 1.0, gate)
        rows = (dot(pick, features) * scale).reshape(EXPERTS, QUAD, 2 * PAIR)
        out_ref[:, q] = rows.astype(BF)


def table_kernel(ids_ref, gates_ref, pick_ref, gate_ref):
    firsts = [QUAD * q for q in range(2 * QUADS)]
    for i, (pick, gate) in enumerate(slot_table(ids_ref, gates_ref, firsts)):
        half, q = i // QUADS, i % QUADS
        pick_ref[half, q * QROWS : (q + 1) * QROWS] = pick
        gate_ref[half, q * QROWS : (q + 1) * QROWS] = gate


def sums_kernel(quads, gate, up, down, rows_hbm, out_hbm, rows, out, sems):
    columns = [pl.ds(i * FFW, FFW) for i in range(3)]
    stores = copies_of([(out.at[:, c], out_hbm.at[:, c]) for c in columns], sems)
    for q in range(QUADS):
        block = quads[:, q].astype(F32).reshape(QROWS, 2 * PAIR).astype(BF)
        for y in range(N_Y):
            at = y * SHARD + q * PIECE
            rows[at : at + PIECE] = block[y * PIECE : (y + 1) * PIECE]
    rows_store = pltpu.make_async_copy(rows, rows_hbm, sems.at[3])
    rows_store.start()
    for i, weights in enumerate((gate, up, down)):
        left = rows[:, :STACK] if i < 2 else rows[:, 2 * PAIR - STACK :]
        out[:, i * FFW : (i + 1) * FFW] = dot(left, weights[...]).astype(BF)
        stores[i].start()
    wait(stores + [rows_store])


def shard_kernel(sums_hbm, main_hbm, last_ref, sums, main, in_sem, out_sem):
    load = pltpu.make_async_copy(sums_hbm, sums, in_sem.at[0])
    store = pltpu.make_async_copy(main, main_hbm, out_sem.at[0])
    load.start()
    load.wait()
    gate_sum, up_sum, total = [sums[:, i * FFW : (i + 1) * FFW].astype(F32) for i in range(3)]
    logistic = jax.nn.sigmoid(gate_sum)
    silu = gate_sum * logistic
    slope = logistic * (1.0 + gate_sum * (1.0 - logistic))
    results = [silu * up_sum, total * up_sum * slope, total * silu]
    cut = SHARD - PIECE
    for i, result in enumerate(results):
        main[:, i * FFW : (i + 1) * FFW] = result[:cut].astype(BF)
    store.start()
    for i, result in enumerate(results):
        last_ref[:, i * FFW : (i + 1) * FFW] = result[cut:].astype(BF)
    store.wait()


def back_parts(full, weights):
    grad = dot_t(full[:, FFW : 2 * FFW], weights[1]) + dot_t(full[:, 2 * FFW :], weights[2])
    return [grad, dot_t(full[:, :FFW], weights[0])]


def back_kernel(full_hbm, gate_hbm, up_hbm, down_hbm, out_ref, full, weights, sems):
    size = full.shape[1] // N_Y
    loads = copies_of(
        [(w, weights.at[i]) for i, w in enumerate((down_hbm, gate_hbm, up_hbm))]
        + [
            (full_hbm.at[pl.ds((2 * y + half) * size, size)], full.at[half, pl.ds(y * size, size)])
            for half in range(2)
            for y in range(N_Y)
        ],
        sems,
    )
    start(loads)
    wait(loads[:3])
    parts = []
    for half in range(2):
        wait(loads[3 + half * N_Y : 3 + (half + 1) * N_Y])
        parts += back_parts(full.at[half], weights)
    result = jnp.concatenate(parts, axis=1)
    for q in range(MAIN):
        starts = [y * size + q * PIECE for y in range(N_Y)]
        block = jnp.concatenate([result[at : at + PIECE] for at in starts], axis=0)
        out_ref[:, q] = block.reshape(EXPERTS, QUAD, 2 * PAIR).astype(BF)


def back_last_kernel(full, gate, up, down, out_ref):
    result = dot_t(full[:, :FFW], down[...])
    grad = dot_t(full[:, FFW : 2 * FFW], gate[...]) + dot_t(full[:, 2 * FFW :], up[...])
    middle = grad[:, JOIN:] + result[:, : STACK - JOIN]
    rows = jnp.concatenate([grad[:, :JOIN], middle, result[:, STACK - JOIN :]], axis=1)
    out_ref[:, 0] = rows.reshape(EXPERTS, QUAD, 2 * PAIR).astype(BF)


def grads_kernel(*refs):
    hbm, (gate_ref, up_ref, down_ref), bufs, sems = refs[:6], refs[6:9], refs[9:15], refs[15]
    full_hbm, full = hbm[0], bufs[0]
    columns = [pl.ds(i * FFW, FFW) for i in range(3)]
    pairs = list(zip(hbm[1:], bufs[1:])) + [(full_hbm.at[:, c], full.at[:, c]) for c in columns]
    loads = copies_of(pairs, sems)
    start(loads)
    wait(loads[:5])
    for i, (out, first) in enumerate(((down_ref, WIDE), (gate_ref, 0), (up_ref, 0))):
        loads[5 + i].wait()
        total = 0.0
        for sums, rows in zip(bufs[:3], bufs[3:]):
            total = total + t_dot(rows[:, first : first + WIDE], sums[:, columns[i]])
        out[...] = total.astype(BF)


def gated_sum(pick, scaled):
    high = scaled.astype(BF)
    low = (scaled - high.astype(F32)).astype(BF)
    return t_dot(pick, high) + t_dot(pick, low)


def mix_last_kernel(core_ref, pick_ref, gate_ref, last_ref, out_ref):
    back = last_ref[:, 0].astype(F32).reshape(QROWS, 2 * PAIR)
    rows = pl.ds(MAIN * QROWS, QROWS)
    scale = jnp.where(iota((1, 2 * PAIR), 1) < PAIR, 1.0, gate_ref[core_ref[0], rows])
    out_ref[...] = gated_sum(pick_ref[core_ref[0], rows], back * scale)


def mix_kernel(pick_ref, gate_ref, main_ref, own_ref, other_ref, grad_ref, mixed_ref):
    quads = [main_ref[:, q] for q in range(MAIN)]
    back = jnp.concatenate([q.astype(F32).reshape(QROWS, 2 * PAIR) for q in quads], axis=0)
    rows = slice(0, MAIN * QROWS)
    totals = []
    for half in range(2):
        skip = half * (PAIR - JOIN)
        lane = iota((1, STACK), 1)
        scale = jnp.where(lane < skip + WIDE, 1.0, gate_ref[half, rows])
        scaled = back[:, half * JOIN : half * JOIN + STACK] * scale
        totals.append(gated_sum(pick_ref[half, rows], scaled))
    total = totals[0][:, :PAIR] + totals[1][:, STACK - PAIR :]
    own, other = own_ref[...], other_ref[...]
    grad = total[:, :WIDE] + own[:, :WIDE] + other[:, WIDE:PAIR]
    mixed = total[:, WIDE:] + own[:, PAIR : PAIR + WIDE] + other[:, PAIR + WIDE :]
    grad_ref[...] = grad.astype(BF)
    mixed_ref[...] = mixed.astype(BF)


HBM_SPEC = pl.BlockSpec(memory_space=pltpu.HBM)
VMEM_SPEC = pl.BlockSpec(memory_space=pltpu.VMEM)
SMEM_SPEC = pl.BlockSpec(memory_space=pltpu.SMEM)


def call(kernel, out_shape, *args, **kwargs):
    return pl.pallas_call(
        kernel,
        out_shape=out_shape,
        compiler_params=pltpu.CompilerParams(vmem_limit_bytes=VMEM_LIMIT),
        name=kernel.__name__,
        **kwargs,
    )(*args)


def in_hbm(*arrays):
    return [pltpu.with_memory_space_constraint(a, pltpu.HBM) for a in arrays]


def in_vmem(*arrays):
    return [pltpu.with_memory_space_constraint(a, pltpu.VMEM) for a in arrays]


def buffers(*arrays):
    return [pltpu.VMEM(a.shape, a.dtype) for a in arrays]


def semaphores(*counts):
    return [pltpu.SemaphoreType.DMA((n,)) for n in counts]


def across(quads, axis):
    return lax.all_to_all(quads, axis, split_axis=0, concat_axis=0, tiled=True)


def swap(array):
    return lax.ppermute(array, "core", [(0, 1), (1, 0)])


def after(array, *others):
    return lax.optimization_barrier((array,) + others)[0]


def split_features(rows):
    own = jnp.concatenate([rows[:, :WIDE], rows[:, PAIR : PAIR + WIDE]], axis=1)
    other = jnp.concatenate([rows[:, WIDE:PAIR], rows[:, PAIR + WIDE :]], axis=1)
    return own, other


def body(tokens, expert_ids, gate_weights, w_gate, w_up, w_down, cotangent):
    gate_own, up_own, down_own = w_gate[0], w_up[0], w_down[0].T
    core = lax.axis_index("core")
    others = swap(jnp.concatenate([tokens, cotangent], axis=0))
    ids, gates = expert_ids.T, gate_weights.T
    inputs = (ids, gates, tokens, cotangent)
    send = call(
        send_kernel,
        shape(EXPERTS, QUADS, QUAD, 2 * PAIR),
        core.reshape(1),
        others,
        *in_hbm(*inputs),
        in_specs=[SMEM_SPEC, VMEM_SPEC] + [HBM_SPEC] * 4,
        scratch_shapes=buffers(*inputs) + semaphores(4),
    )
    quads = across(send, "expert")
    gate_sent, up_sent, down_sent, _ = lax.optimization_barrier((gate_own, up_own, down_own, send))
    zeros = jnp.zeros((STACK - PAIR, FFW), BF)
    stacks = (
        jnp.concatenate([gate_sent, swap(gate_sent), zeros], axis=0),
        jnp.concatenate([up_sent, swap(up_sent), zeros], axis=0),
        jnp.concatenate([zeros, down_sent, swap(down_sent)], axis=0),
    )
    rows, parts = call(
        sums_kernel,
        [pltpu.HBM((ROWS, 2 * PAIR), BF), pltpu.HBM((ROWS, 3 * FFW), BF)],
        quads,
        *in_vmem(*stacks),
        in_specs=[VMEM_SPEC] * 4,
        out_specs=[HBM_SPEC] * 2,
        scratch_shapes=[pltpu.VMEM((ROWS, 2 * PAIR), BF), pltpu.VMEM((ROWS, 3 * FFW), BF)]
        + semaphores(4),
    )
    sums = lax.psum_scatter(parts, "y", scatter_dimension=0, tiled=True)

    rows, ids, gates, _ = lax.optimization_barrier((rows, ids, gates, parts))
    pick, slot_gate = call(
        table_kernel,
        [shape(2, ROWS, tokens.shape[0]), shape(2, ROWS, 1, dtype=F32)],
        ids,
        gates,
    )
    own, other = split_features(rows)
    other = swap(other)
    own, other = own.reshape(N_Y, SHARD, PAIR), other.reshape(N_Y, SHARD, PAIR)
    cut = SHARD - PIECE
    own_last = own[:, cut:].reshape(QROWS, PAIR)
    other_last = other[:, cut:].reshape(QROWS, PAIR)
    first = jnp.where(core == 0, own, other)[:, None, :cut]
    second = jnp.where(core == 0, other, own)[:, None, :cut]
    main = jnp.concatenate([first, second], axis=1).reshape(2 * MAIN * QROWS, PAIR)
    sums, main, own_last, other_last, pick, slot_gate = lax.optimization_barrier(
        (sums, main, own_last, other_last, pick, slot_gate)
    )

    shard_shape = shape(cut, 3 * FFW)
    shard, shard_last = call(
        shard_kernel,
        [pltpu.HBM((cut, 3 * FFW), BF), shape(PIECE, 3 * FFW)],
        *in_hbm(sums),
        in_specs=[HBM_SPEC],
        out_specs=[HBM_SPEC, VMEM_SPEC],
        scratch_shapes=buffers(sums, shard_shape) + semaphores(1, 1),
    )
    full = lax.all_gather(shard, ("y", "core"), axis=0, tiled=True)

    full_last = lax.all_gather(shard_last, "y", axis=0, tiled=True)
    send_last = call(
        back_last_kernel, shape(EXPERTS, 1, QUAD, 2 * PAIR), full_last, *in_vmem(*stacks)
    )
    back_last = across(send_last, "expert")
    full_other = swap(after(full_last, send_last))

    back = call(
        back_kernel,
        shape(EXPERTS, MAIN, QUAD, 2 * PAIR),
        *in_hbm(full, gate_own, up_own, down_own),
        in_specs=[HBM_SPEC] * 4,
        out_specs=VMEM_SPEC,
        scratch_shapes=[
            pltpu.VMEM((2, MAIN * QROWS, 3 * FFW), BF),
            pltpu.VMEM((3, WIDE, FFW), BF),
        ]
        + semaphores(3 + 2 * N_Y),
    )
    grad_inputs = (full, full_last, full_other, after(main, back), own_last, other_last)
    grads = call(
        grads_kernel,
        [shape(WIDE, FFW)] * 3,
        *in_hbm(*grad_inputs),
        in_specs=[HBM_SPEC] * 6,
        scratch_shapes=buffers(*grad_inputs) + semaphores(8),
    )
    back = across(back, "expert")
    back_last = after(back_last, grads[2])
    total_last = call(
        mix_last_kernel,
        shape(tokens.shape[0], 2 * PAIR, dtype=F32),
        core.reshape(1),
        pick,
        slot_gate,
        back_last,
        in_specs=[SMEM_SPEC] + [VMEM_SPEC] * 3,
    )
    other_total = swap(total_last)
    back = after(back, other_total, *grads)
    token_grad, mixed = call(
        mix_kernel, [shape(*tokens.shape)] * 2, pick, slot_gate, back, total_last, other_total
    )
    return mixed, token_grad, grads[0][None], grads[1][None], grads[2].T[None]


def solution(mesh):
    fine = Mesh(mesh.devices.reshape(N_Y, 2, EXPERTS), ("y", "core", "expert"))
    dp = ("y", "core")
    placed = (
        P("expert", dp),
        P("expert", None),
        P("expert", None),
        P("expert", dp, None),
        P("expert", dp, None),
        P("expert", None, dp),
        P("expert", dp),
    )
    return jax.shard_map(
        body,
        mesh=fine,
        in_specs=placed,
        out_specs=(
            P("expert", dp),
            P("expert", dp),
            P("expert", dp, None),
            P("expert", dp, None),
            P("expert", None, dp),
        ),
        check_vma=False,
    )
```

```python
import jax
import jax.numpy as jnp
from jax import lax
from jax.experimental import pallas as pl
from jax.experimental.pallas import tpu as pltpu
from jax.sharding import Mesh, PartitionSpec as P

EXPERTS = 32
CAP = 32
HALF = CAP // 2
QUAD = 4
QUADS = HALF // QUAD
MAIN = QUADS - 1
QROWS = EXPERTS * QUAD
ROWS = QUADS * QROWS
WIDE = 224
PAIR = 2 * WIDE
STACK = 512
JOIN = 2 * PAIR - STACK
FFW = 1024
N_Y = 8
PIECE = QROWS // N_Y
SHARD = ROWS // N_Y
BF = jnp.bfloat16
F32 = jnp.float32
VMEM_LIMIT = 24 * 1024 * 1024


def iota(shape, dim):
    return lax.broadcasted_iota(jnp.int32, shape, dim)


def dot(left, right):
    return jnp.dot(left, right, preferred_element_type=F32)


def dot_t(left, right):
    return lax.dot_general(left, right, (((1,), (1,)), ((), ())), preferred_element_type=F32)


def t_dot(left, right):
    return lax.dot_general(left, right, (((0,), (0,)), ((), ())), preferred_element_type=F32)


def shape(*dims, dtype=BF):
    return jax.ShapeDtypeStruct(dims, dtype)


def start(copies):
    for copy in copies:
        copy.start()


def wait(copies):
    for copy in copies:
        copy.wait()


def copies_of(pairs, sems):
    return [pltpu.make_async_copy(src, dst, sems.at[i]) for i, (src, dst) in enumerate(pairs)]


def slot_table(ids_ref, gates_ref, firsts):
    tokens = ids_ref.shape[1]
    numbers = iota((EXPERTS, tokens), 0)
    chosen = jnp.zeros((EXPERTS, tokens), F32)
    weight = jnp.zeros((EXPERTS, tokens), F32)
    for k in range(ids_ref.shape[0]):
        hit = ids_ref[k : k + 1, :] == numbers
        chosen = chosen + jnp.where(hit, 1.0, 0.0)
        weight = weight + jnp.where(hit, gates_ref[k : k + 1, :], 0.0)
    earlier = jnp.where(iota((tokens, tokens), 0) < iota((tokens, tokens), 1), 1.0, 0.0)
    rank = dot(chosen.astype(BF), earlier.astype(BF))
    rank = jnp.where(chosen > 0.5, rank, -1.0).astype(jnp.int32)
    tables = []
    for first in firsts:
        hit = (rank - first)[:, None, :] == iota((EXPERTS, QUAD, tokens), 1)
        pick = jnp.where(hit, 1.0, 0.0).reshape(QROWS, tokens)
        gate = jnp.where(hit, weight[:, None, :], 0.0).reshape(QROWS, tokens)
        tables.append((pick.astype(BF), jnp.sum(gate, axis=1, keepdims=True)))
    return tables


def send_kernel(
    core_ref,
    others_ref,
    ids_hbm,
    gates_hbm,
    tokens_hbm,
    cotangent_hbm,
    out_ref,
    ids_ref,
    gates_ref,
    tokens_ref,
    cotangent_ref,
    sems,
):
    loads = copies_of(
        (
            (ids_hbm, ids_ref),
            (gates_hbm, gates_ref),
            (tokens_hbm, tokens_ref),
            (cotangent_hbm, cotangent_ref),
        ),
        sems,
    )
    start(loads)
    wait(loads[:2])
    firsts = [core_ref[0] * HALF + QUAD * q for q in range(QUADS)]
    tables = slot_table(ids_ref, gates_ref, firsts)
    wait(loads[2:])
    count = tokens_ref.shape[0]
    features = jnp.concatenate(
        [tokens_ref[...], others_ref[:count], cotangent_ref[...], others_ref[count:]], axis=1
    )
    for q, (pick, gate) in enumerate(tables):
        scale = jnp.where(iota((1, 2 * PAIR), 1) < PAIR, 1.0, gate)
        rows = (dot(pick, features) * scale).reshape(EXPERTS, QUAD, 2 * PAIR)
        out_ref[:, q] = rows.astype(BF)


def table_kernel(ids_ref, gates_ref, pick_ref, gated_ref):
    firsts = [QUAD * q for q in range(2 * QUADS)]
    for i, (pick, gate) in enumerate(slot_table(ids_ref, gates_ref, firsts)):
        half, q = i // QUADS, i % QUADS
        pick_ref[half, q * QROWS : (q + 1) * QROWS] = pick
        gated_ref[half, q * QROWS : (q + 1) * QROWS] = (pick.astype(F32) * gate).astype(BF)


def sums_kernel(quads, gate, up, down, rows_hbm, out_hbm, rows, out, sems):
    wide = FFW // 2
    columns = [pl.ds(i * wide, wide) for i in range(6)]
    stores = copies_of([(out.at[:, c], out_hbm.at[:, c]) for c in columns], sems)
    for q in range(QUADS):
        block = quads[:, q].astype(F32).reshape(QROWS, 2 * PAIR).astype(BF)
        for y in range(N_Y):
            at = y * SHARD + q * PIECE
            rows[at : at + PIECE] = block[y * PIECE : (y + 1) * PIECE]
    rows_store = pltpu.make_async_copy(rows, rows_hbm, sems.at[6])
    rows_store.start()
    for i, weights in enumerate((gate, gate, up, up, down, down)):
        left = rows[:, :STACK] if i < 4 else rows[:, 2 * PAIR - STACK :]
        right = weights[:, i % 2 * wide : (i % 2 + 1) * wide]
        out[:, i * wide : (i + 1) * wide] = dot(left, right).astype(BF)
        stores[i].start()
    wait(stores + [rows_store])


def shard_kernel(sums_hbm, main_hbm, last_ref, sums, main, in_sem, out_sem):
    load = pltpu.make_async_copy(sums_hbm, sums, in_sem.at[0])
    store = pltpu.make_async_copy(main, main_hbm, out_sem.at[0])
    load.start()
    load.wait()
    gate_sum, up_sum, total = [sums[:, i * FFW : (i + 1) * FFW].astype(F32) for i in range(3)]
    logistic = jax.nn.sigmoid(gate_sum)
    silu = gate_sum * logistic
    slope = logistic * (1.0 + gate_sum * (1.0 - logistic))
    results = [silu * up_sum, total * up_sum * slope, total * silu]
    cut = SHARD - PIECE
    for i, result in enumerate(results):
        main[:, i * FFW : (i + 1) * FFW] = result[:cut].astype(BF)
    store.start()
    for i, result in enumerate(results):
        last_ref[:, i * FFW : (i + 1) * FFW] = result[cut:].astype(BF)
    store.wait()


def back_parts(full, weights):
    grad = dot_t(full[:, FFW : 2 * FFW], weights[1]) + dot_t(full[:, 2 * FFW :], weights[2])
    return [grad, dot_t(full[:, :FFW], weights[0])]


def back_kernel(full_hbm, gate_hbm, up_hbm, down_hbm, out_ref, full, weights, sems):
    size = full.shape[1] // N_Y
    loads = copies_of(
        [(w, weights.at[i]) for i, w in enumerate((down_hbm, gate_hbm, up_hbm))]
        + [
            (full_hbm.at[pl.ds((2 * y + half) * size, size)], full.at[half, pl.ds(y * size, size)])
            for half in range(2)
            for y in range(N_Y)
        ],
        sems,
    )
    start(loads)
    wait(loads[:3])
    parts = []
    for half in range(2):
        wait(loads[3 + half * N_Y : 3 + (half + 1) * N_Y])
        parts += back_parts(full.at[half], weights)
    result = jnp.concatenate(parts, axis=1)
    for q in range(MAIN):
        starts = [y * size + q * PIECE for y in range(N_Y)]
        block = jnp.concatenate([result[at : at + PIECE] for at in starts], axis=0)
        out_ref[:, q] = block.reshape(EXPERTS, QUAD, 2 * PAIR).astype(BF)


def back_last_kernel(full, gate, up, down, out_ref):
    result = dot_t(full[:, :FFW], down[...])
    grad = dot_t(full[:, FFW : 2 * FFW], gate[...]) + dot_t(full[:, 2 * FFW :], up[...])
    middle = grad[:, JOIN:] + result[:, : STACK - JOIN]
    rows = jnp.concatenate([grad[:, :JOIN], middle, result[:, STACK - JOIN :]], axis=1)
    out_ref[:, 0] = rows.reshape(EXPERTS, QUAD, 2 * PAIR).astype(BF)


def grads_kernel(*refs):
    hbm, (gate_ref, up_ref, down_ref), bufs, sems = refs[:6], refs[6:9], refs[9:15], refs[15]
    full_hbm, full = hbm[0], bufs[0]
    columns = [pl.ds(i * FFW, FFW) for i in range(3)]
    pairs = list(zip(hbm[1:], bufs[1:])) + [(full_hbm.at[:, c], full.at[:, c]) for c in columns]
    loads = copies_of(pairs, sems)
    start(loads)
    wait(loads[:5])
    for i, (out, first) in enumerate(((down_ref, WIDE), (gate_ref, 0), (up_ref, 0))):
        loads[5 + i].wait()
        total = 0.0
        for sums, rows in zip(bufs[:3], bufs[3:]):
            total = total + t_dot(rows[:, first : first + WIDE], sums[:, columns[i]])
        out[...] = total.astype(BF)


def mix_last_kernel(core_ref, pick_ref, gated_ref, last_ref, out_ref):
    back = last_ref[:, 0].astype(F32).reshape(QROWS, 2 * PAIR).astype(BF)
    rows = pl.ds(MAIN * QROWS, QROWS)
    plain = t_dot(pick_ref[core_ref[0], rows], back)
    gated = t_dot(gated_ref[core_ref[0], rows], back)
    out_ref[...] = jnp.where(iota((1, 2 * PAIR), 1) < PAIR, plain, gated)


def mix_kernel(pick_ref, gated_ref, main_ref, own_ref, other_ref, grad_ref, mixed_ref):
    quads = [main_ref[:, q] for q in range(MAIN)]
    quads = [q.astype(F32).reshape(QROWS, 2 * PAIR).astype(BF) for q in quads]
    back = jnp.concatenate(quads, axis=0)
    rows = slice(0, MAIN * QROWS)
    totals = []
    for half in range(2):
        columns = back[:, half * JOIN : half * JOIN + STACK]
        plain = t_dot(pick_ref[half, rows], columns)
        gated = t_dot(gated_ref[half, rows], columns)
        skip = half * (PAIR - JOIN)
        totals.append(jnp.where(iota((1, STACK), 1) < skip + WIDE, plain, gated))
    total = totals[0][:, :PAIR] + totals[1][:, STACK - PAIR :]
    own, other = own_ref[...], other_ref[...]
    grad = total[:, :WIDE] + own[:, :WIDE] + other[:, WIDE:PAIR]
    mixed = total[:, WIDE:] + own[:, PAIR : PAIR + WIDE] + other[:, PAIR + WIDE :]
    grad_ref[...] = grad.astype(BF)
    mixed_ref[...] = mixed.astype(BF)


HBM_SPEC = pl.BlockSpec(memory_space=pltpu.HBM)
VMEM_SPEC = pl.BlockSpec(memory_space=pltpu.VMEM)
SMEM_SPEC = pl.BlockSpec(memory_space=pltpu.SMEM)


def call(kernel, out_shape, *args, **kwargs):
    return pl.pallas_call(
        kernel,
        out_shape=out_shape,
        compiler_params=pltpu.CompilerParams(vmem_limit_bytes=VMEM_LIMIT),
        name=kernel.__name__,
        **kwargs,
    )(*args)


def in_hbm(*arrays):
    return [pltpu.with_memory_space_constraint(a, pltpu.HBM) for a in arrays]


def in_vmem(*arrays):
    return [pltpu.with_memory_space_constraint(a, pltpu.VMEM) for a in arrays]


def buffers(*arrays):
    return [pltpu.VMEM(a.shape, a.dtype) for a in arrays]


def semaphores(*counts):
    return [pltpu.SemaphoreType.DMA((n,)) for n in counts]


def across(quads, axis):
    return lax.all_to_all(quads, axis, split_axis=0, concat_axis=0, tiled=True)


def swap(array):
    return lax.ppermute(array, "core", [(0, 1), (1, 0)])


def after(array, *others):
    return lax.optimization_barrier((array,) + others)[0]


def split_features(rows):
    own = jnp.concatenate([rows[:, :WIDE], rows[:, PAIR : PAIR + WIDE]], axis=1)
    other = jnp.concatenate([rows[:, WIDE:PAIR], rows[:, PAIR + WIDE :]], axis=1)
    return own, other


def body(tokens, expert_ids, gate_weights, w_gate, w_up, w_down, cotangent):
    gate_own, up_own, down_own = w_gate[0], w_up[0], w_down[0].T
    core = lax.axis_index("core")
    others = swap(jnp.concatenate([tokens, cotangent], axis=0))
    ids, gates = expert_ids.T, gate_weights.T
    inputs = (ids, gates, tokens, cotangent)
    send = call(
        send_kernel,
        shape(EXPERTS, QUADS, QUAD, 2 * PAIR),
        core.reshape(1),
        others,
        *in_hbm(*inputs),
        in_specs=[SMEM_SPEC, VMEM_SPEC] + [HBM_SPEC] * 4,
        scratch_shapes=buffers(*inputs) + semaphores(4),
    )
    quads = across(send, "expert")
    gate_sent, up_sent, down_sent, _ = lax.optimization_barrier((gate_own, up_own, down_own, send))
    zeros = jnp.zeros((STACK - PAIR, FFW), BF)
    stacks = (
        jnp.concatenate([gate_sent, swap(gate_sent), zeros], axis=0),
        jnp.concatenate([up_sent, swap(up_sent), zeros], axis=0),
        jnp.concatenate([zeros, down_sent, swap(down_sent)], axis=0),
    )
    rows, parts = call(
        sums_kernel,
        [pltpu.HBM((ROWS, 2 * PAIR), BF), pltpu.HBM((ROWS, 3 * FFW), BF)],
        quads,
        *in_vmem(*stacks),
        in_specs=[VMEM_SPEC] * 4,
        out_specs=[HBM_SPEC] * 2,
        scratch_shapes=[pltpu.VMEM((ROWS, 2 * PAIR), BF), pltpu.VMEM((ROWS, 3 * FFW), BF)]
        + semaphores(7),
    )
    sums = lax.psum_scatter(parts, "y", scatter_dimension=0, tiled=True)

    rows, ids, gates, _ = lax.optimization_barrier((rows, ids, gates, parts))
    pick, gated = call(
        table_kernel,
        [shape(2, ROWS, tokens.shape[0])] * 2,
        ids,
        gates,
    )
    own, other = split_features(rows)
    other = swap(other)
    own, other = own.reshape(N_Y, SHARD, PAIR), other.reshape(N_Y, SHARD, PAIR)
    cut = SHARD - PIECE
    own_last = own[:, cut:].reshape(QROWS, PAIR)
    other_last = other[:, cut:].reshape(QROWS, PAIR)
    first = jnp.where(core == 0, own, other)[:, None, :cut]
    second = jnp.where(core == 0, other, own)[:, None, :cut]
    main = jnp.concatenate([first, second], axis=1).reshape(2 * MAIN * QROWS, PAIR)
    sums, main, own_last, other_last, pick, gated = lax.optimization_barrier(
        (sums, main, own_last, other_last, pick, gated)
    )

    shard_shape = shape(cut, 3 * FFW)
    shard, shard_last = call(
        shard_kernel,
        [pltpu.HBM((cut, 3 * FFW), BF), shape(PIECE, 3 * FFW)],
        *in_hbm(sums),
        in_specs=[HBM_SPEC],
        out_specs=[HBM_SPEC, VMEM_SPEC],
        scratch_shapes=buffers(sums, shard_shape) + semaphores(1, 1),
    )
    full = lax.all_gather(shard, ("y", "core"), axis=0, tiled=True)

    full_last = lax.all_gather(shard_last, "y", axis=0, tiled=True)
    send_last = call(
        back_last_kernel, shape(EXPERTS, 1, QUAD, 2 * PAIR), full_last, *in_vmem(*stacks)
    )
    back_last = across(send_last, "expert")
    full_other = swap(after(full_last, send_last))

    back = call(
        back_kernel,
        shape(EXPERTS, MAIN, QUAD, 2 * PAIR),
        *in_hbm(full, gate_own, up_own, down_own),
        in_specs=[HBM_SPEC] * 4,
        out_specs=VMEM_SPEC,
        scratch_shapes=[
            pltpu.VMEM((2, MAIN * QROWS, 3 * FFW), BF),
            pltpu.VMEM((3, WIDE, FFW), BF),
        ]
        + semaphores(3 + 2 * N_Y),
    )
    grad_inputs = (full, full_last, full_other, after(main, back), own_last, other_last)
    grads = call(
        grads_kernel,
        [shape(WIDE, FFW)] * 3,
        *in_hbm(*grad_inputs),
        in_specs=[HBM_SPEC] * 6,
        scratch_shapes=buffers(*grad_inputs) + semaphores(8),
    )
    back = across(back, "expert")
    back_last = after(back_last, grads[2])
    total_last = call(
        mix_last_kernel,
        shape(tokens.shape[0], 2 * PAIR, dtype=F32),
        core.reshape(1),
        pick,
        gated,
        back_last,
        in_specs=[SMEM_SPEC] + [VMEM_SPEC] * 3,
    )
    other_total = swap(total_last)
    back = after(back, other_total, *grads)
    token_grad, mixed = call(
        mix_kernel, [shape(*tokens.shape)] * 2, pick, gated, back, total_last, other_total
    )
    return mixed, token_grad, grads[0][None], grads[1][None], grads[2].T[None]


def solution(mesh):
    fine = Mesh(mesh.devices.reshape(N_Y, 2, EXPERTS), ("y", "core", "expert"))
    dp = ("y", "core")
    placed = (
        P("expert", dp),
        P("expert", None),
        P("expert", None),
        P("expert", dp, None),
        P("expert", dp, None),
        P("expert", None, dp),
        P("expert", dp),
    )
    return jax.shard_map(
        body,
        mesh=fine,
        in_specs=placed,
        out_specs=(
            P("expert", dp),
            P("expert", dp),
            P("expert", dp, None),
            P("expert", dp, None),
            P("expert", None, dp),
        ),
        check_vma=False,
    )
```

```python
import jax
import jax.numpy as jnp
from jax import lax
from jax.experimental import pallas as pl
from jax.experimental.pallas import tpu as pltpu
from jax.sharding import Mesh, PartitionSpec as P

EXPERTS = 32
CAP = 32
HALF = CAP // 2
QUAD = 4
QUADS = HALF // QUAD
MAIN = QUADS - 1
QROWS = EXPERTS * QUAD
ROWS = QUADS * QROWS
WIDE = 224
PAIR = 2 * WIDE
STACK = 512
JOIN = 2 * PAIR - STACK
FFW = 1024
N_Y = 8
PIECE = QROWS // N_Y
SHARD = ROWS // N_Y
BF = jnp.bfloat16
F32 = jnp.float32
VMEM_LIMIT = 24 * 1024 * 1024


def iota(shape, dim):
    return lax.broadcasted_iota(jnp.int32, shape, dim)


def dot(left, right):
    return jnp.dot(left, right, preferred_element_type=F32)


def dot_t(left, right):
    return lax.dot_general(left, right, (((1,), (1,)), ((), ())), preferred_element_type=F32)


def t_dot(left, right):
    return lax.dot_general(left, right, (((0,), (0,)), ((), ())), preferred_element_type=F32)


def shape(*dims, dtype=BF):
    return jax.ShapeDtypeStruct(dims, dtype)


def start(copies):
    for copy in copies:
        copy.start()


def wait(copies):
    for copy in copies:
        copy.wait()


def copies_of(pairs, sems):
    return [pltpu.make_async_copy(src, dst, sems.at[i]) for i, (src, dst) in enumerate(pairs)]


def slot_table(ids_ref, gates_ref, firsts):
    tokens = ids_ref.shape[1]
    numbers = iota((EXPERTS, tokens), 0)
    chosen = jnp.zeros((EXPERTS, tokens), F32)
    weight = jnp.zeros((EXPERTS, tokens), F32)
    for k in range(ids_ref.shape[0]):
        hit = ids_ref[k : k + 1, :] == numbers
        chosen = chosen + jnp.where(hit, 1.0, 0.0)
        weight = weight + jnp.where(hit, gates_ref[k : k + 1, :], 0.0)
    earlier = jnp.where(iota((tokens, tokens), 0) < iota((tokens, tokens), 1), 1.0, 0.0)
    rank = dot(chosen.astype(BF), earlier.astype(BF))
    rank = jnp.where(chosen > 0.5, rank, -1.0).astype(jnp.int32)
    tables = []
    for first in firsts:
        hit = (rank - first)[:, None, :] == iota((EXPERTS, QUAD, tokens), 1)
        pick = jnp.where(hit, 1.0, 0.0).reshape(QROWS, tokens)
        gate = jnp.where(hit, weight[:, None, :], 0.0).reshape(QROWS, tokens)
        tables.append((pick.astype(BF), jnp.sum(gate, axis=1, keepdims=True)))
    return tables


def send_kernel(
    ids_hbm,
    gates_hbm,
    tokens_hbm,
    cotangent_hbm,
    out_ref,
    ids_ref,
    gates_ref,
    tokens_ref,
    cotangent_ref,
    sems,
):
    loads = copies_of(
        (
            (ids_hbm, ids_ref),
            (gates_hbm, gates_ref),
            (tokens_hbm, tokens_ref),
            (cotangent_hbm, cotangent_ref),
        ),
        sems,
    )
    start(loads)
    wait(loads[:2])
    tables = slot_table(ids_ref, gates_ref, [QUAD * q for q in range(2 * QUADS)])
    wait(loads[2:])
    features = jnp.concatenate([tokens_ref[...], cotangent_ref[...]], axis=1)
    for pair in range(QUADS):
        rows = []
        for pick, gate in tables[2 * pair : 2 * pair + 2]:
            scale = jnp.where(iota((1, PAIR), 1) < WIDE, 1.0, gate)
            rows.append(dot(pick, features) * scale)
        rows = jnp.concatenate(rows, axis=1).reshape(EXPERTS, QUAD, 2 * PAIR)
        half, place = pair // (QUADS // 2), pair % (QUADS // 2)
        out_ref[half * EXPERTS : (half + 1) * EXPERTS, place] = rows.astype(BF)


def table_kernel(ids_ref, gates_ref, pick_ref, gated_ref):
    firsts = [QUAD * q for q in range(2 * QUADS)]
    for i, (pick, gate) in enumerate(slot_table(ids_ref, gates_ref, firsts)):
        half, q = i // QUADS, i % QUADS
        pick_ref[half, q * QROWS : (q + 1) * QROWS] = pick
        gated_ref[half, q * QROWS : (q + 1) * QROWS] = (pick.astype(F32) * gate).astype(BF)


def sums_kernel(quads, gate, up, down, rows_hbm, out_hbm, rows, out, sems):
    wide = FFW // 2
    columns = [pl.ds(i * wide, wide) for i in range(6)]
    stores = copies_of([(out.at[:, c], out_hbm.at[:, c]) for c in columns], sems)
    for q in range(QUADS):
        pieces = []
        for core in range(2):
            block = quads[core * EXPERTS : (core + 1) * EXPERTS, q // 2].astype(F32)
            block = block.reshape(QROWS, 2 * PAIR)[:, q % 2 * PAIR : (q % 2 + 1) * PAIR]
            pieces.append((block[:, :WIDE], block[:, WIDE:]))
        (in_0, dy_0), (in_1, dy_1) = pieces
        block = jnp.concatenate([in_0, in_1, dy_0, dy_1], axis=1).astype(BF)
        for y in range(N_Y):
            at = y * SHARD + q * PIECE
            rows[at : at + PIECE] = block[y * PIECE : (y + 1) * PIECE]
    rows_store = pltpu.make_async_copy(rows, rows_hbm, sems.at[6])
    rows_store.start()
    for i, weights in enumerate((gate, gate, up, up, down, down)):
        left = rows[:, :STACK] if i < 4 else rows[:, 2 * PAIR - STACK :]
        right = weights[:, i % 2 * wide : (i % 2 + 1) * wide]
        out[:, i * wide : (i + 1) * wide] = dot(left, right).astype(BF)
        stores[i].start()
    wait(stores + [rows_store])


def shard_kernel(sums_hbm, main_hbm, last_ref, sums, main, in_sem, out_sem):
    load = pltpu.make_async_copy(sums_hbm, sums, in_sem.at[0])
    store = pltpu.make_async_copy(main, main_hbm, out_sem.at[0])
    load.start()
    load.wait()
    gate_sum, up_sum, total = [sums[:, i * FFW : (i + 1) * FFW].astype(F32) for i in range(3)]
    logistic = jax.nn.sigmoid(gate_sum)
    silu = gate_sum * logistic
    slope = logistic * (1.0 + gate_sum * (1.0 - logistic))
    results = [silu * up_sum, total * up_sum * slope, total * silu]
    cut = SHARD - PIECE
    for i, result in enumerate(results):
        main[:, i * FFW : (i + 1) * FFW] = result[:cut].astype(BF)
    store.start()
    for i, result in enumerate(results):
        last_ref[:, i * FFW : (i + 1) * FFW] = result[cut:].astype(BF)
    store.wait()


def back_parts(full, weights):
    grad = dot_t(full[:, FFW : 2 * FFW], weights[1]) + dot_t(full[:, 2 * FFW :], weights[2])
    return [grad, dot_t(full[:, :FFW], weights[0])]


def back_kernel(full_hbm, gate_hbm, up_hbm, down_hbm, out_ref, full, weights, sems):
    size = full.shape[1] // N_Y
    loads = copies_of(
        [(w, weights.at[i]) for i, w in enumerate((down_hbm, gate_hbm, up_hbm))]
        + [
            (full_hbm.at[pl.ds((2 * y + half) * size, size)], full.at[half, pl.ds(y * size, size)])
            for half in range(2)
            for y in range(N_Y)
        ],
        sems,
    )
    start(loads)
    wait(loads[:3])
    parts = []
    for half in range(2):
        wait(loads[3 + half * N_Y : 3 + (half + 1) * N_Y])
        parts += back_parts(full.at[half], weights)
    result = jnp.concatenate(parts, axis=1)
    for q in range(MAIN):
        starts = [y * size + q * PIECE for y in range(N_Y)]
        block = jnp.concatenate([result[at : at + PIECE] for at in starts], axis=0)
        out_ref[:, q] = block.reshape(EXPERTS, QUAD, 2 * PAIR).astype(BF)


def back_last_kernel(full, gate, up, down, out_ref):
    result = dot_t(full[:, :FFW], down[...])
    grad = dot_t(full[:, FFW : 2 * FFW], gate[...]) + dot_t(full[:, 2 * FFW :], up[...])
    middle = grad[:, JOIN:] + result[:, : STACK - JOIN]
    rows = jnp.concatenate([grad[:, :JOIN], middle, result[:, STACK - JOIN :]], axis=1)
    out_ref[:, 0] = rows.reshape(EXPERTS, QUAD, 2 * PAIR).astype(BF)


def grads_kernel(*refs):
    hbm, (gate_ref, up_ref, down_ref), bufs, sems = refs[:6], refs[6:9], refs[9:15], refs[15]
    full_hbm, full = hbm[0], bufs[0]
    columns = [pl.ds(i * FFW, FFW) for i in range(3)]
    pairs = list(zip(hbm[1:], bufs[1:])) + [(full_hbm.at[:, c], full.at[:, c]) for c in columns]
    loads = copies_of(pairs, sems)
    start(loads)
    wait(loads[:5])
    for i, (out, first) in enumerate(((down_ref, WIDE), (gate_ref, 0), (up_ref, 0))):
        loads[5 + i].wait()
        total = 0.0
        for sums, rows in zip(bufs[:3], bufs[3:]):
            total = total + t_dot(rows[:, first : first + WIDE], sums[:, columns[i]])
        out[...] = total.astype(BF)


def mix_last_kernel(core_ref, pick_ref, gated_ref, last_ref, out_ref):
    back = last_ref[:, 0].astype(F32).reshape(QROWS, 2 * PAIR).astype(BF)
    rows = pl.ds(MAIN * QROWS, QROWS)
    plain = t_dot(pick_ref[core_ref[0], rows], back)
    gated = t_dot(gated_ref[core_ref[0], rows], back)
    out_ref[...] = jnp.where(iota((1, 2 * PAIR), 1) < PAIR, plain, gated)


def mix_kernel(core_ref, pick_ref, gated_ref, main_ref, own_ref, other_ref, grad_ref, mixed_ref):
    quads = [main_ref[:, q] for q in range(MAIN)]
    quads = [q.astype(F32).reshape(QROWS, 2 * PAIR).astype(BF) for q in quads]
    back = jnp.concatenate(quads, axis=0)
    rows = slice(0, MAIN * QROWS)
    totals = []
    for half in range(2):
        columns = back[:, half * JOIN : half * JOIN + STACK]
        plain = t_dot(pick_ref[half, rows], columns)
        gated = t_dot(gated_ref[half, rows], columns)
        skip = half * (PAIR - JOIN)
        totals.append(jnp.where(iota((1, STACK), 1) < skip + WIDE, plain, gated))
    total = totals[0][:, :PAIR] + totals[1][:, STACK - PAIR :]
    last = own_ref[...] + other_ref[...]
    is_first = core_ref[0] == 0
    grad = total[:, :WIDE] + jnp.where(is_first, last[:, :WIDE], last[:, WIDE:PAIR])
    last = jnp.where(is_first, last[:, PAIR : PAIR + WIDE], last[:, PAIR + WIDE :])
    grad_ref[...] = grad.astype(BF)
    mixed_ref[...] = (total[:, WIDE:] + last).astype(BF)


HBM_SPEC = pl.BlockSpec(memory_space=pltpu.HBM)
VMEM_SPEC = pl.BlockSpec(memory_space=pltpu.VMEM)
SMEM_SPEC = pl.BlockSpec(memory_space=pltpu.SMEM)


def call(kernel, out_shape, *args, **kwargs):
    return pl.pallas_call(
        kernel,
        out_shape=out_shape,
        compiler_params=pltpu.CompilerParams(vmem_limit_bytes=VMEM_LIMIT),
        name=kernel.__name__,
        **kwargs,
    )(*args)


def in_hbm(*arrays):
    return [pltpu.with_memory_space_constraint(a, pltpu.HBM) for a in arrays]


def in_vmem(*arrays):
    return [pltpu.with_memory_space_constraint(a, pltpu.VMEM) for a in arrays]


def buffers(*arrays):
    return [pltpu.VMEM(a.shape, a.dtype) for a in arrays]


def semaphores(*counts):
    return [pltpu.SemaphoreType.DMA((n,)) for n in counts]


def across(quads, axis):
    return lax.all_to_all(quads, axis, split_axis=0, concat_axis=0, tiled=True)


def swap(array):
    return lax.ppermute(array, "core", [(0, 1), (1, 0)])


def after(array, *others):
    return lax.optimization_barrier((array,) + others)[0]


def by_core(core, own, other):
    return jnp.where(core == 0, own, other), jnp.where(core == 0, other, own)


def split_features(core, rows):
    first = jnp.concatenate([rows[:, :WIDE], rows[:, PAIR : PAIR + WIDE]], axis=1)
    second = jnp.concatenate([rows[:, WIDE:PAIR], rows[:, PAIR + WIDE :]], axis=1)
    return by_core(core, first, second)


def body(tokens, expert_ids, gate_weights, w_gate, w_up, w_down, cotangent):
    gate_own, up_own, down_own = w_gate[0], w_up[0], w_down[0].T
    core = lax.axis_index("core")
    ids, gates = expert_ids.T, gate_weights.T
    inputs = (ids, gates, tokens, cotangent)
    send = call(
        send_kernel,
        shape(2 * EXPERTS, QUADS // 2, QUAD, 2 * PAIR),
        *in_hbm(*inputs),
        in_specs=[HBM_SPEC] * 4,
        scratch_shapes=buffers(*inputs) + semaphores(4),
    )
    quads = across(send, ("core", "expert"))
    gate_sent, up_sent, down_sent, _ = lax.optimization_barrier((gate_own, up_own, down_own, send))
    zeros = jnp.zeros((STACK - PAIR, FFW), BF)
    stacks = (
        jnp.concatenate([*by_core(core, gate_sent, swap(gate_sent)), zeros], axis=0),
        jnp.concatenate([*by_core(core, up_sent, swap(up_sent)), zeros], axis=0),
        jnp.concatenate([zeros, *by_core(core, down_sent, swap(down_sent))], axis=0),
    )
    rows, parts = call(
        sums_kernel,
        [pltpu.HBM((ROWS, 2 * PAIR), BF), pltpu.HBM((ROWS, 3 * FFW), BF)],
        quads,
        *in_vmem(*stacks),
        in_specs=[VMEM_SPEC] * 4,
        out_specs=[HBM_SPEC] * 2,
        scratch_shapes=[pltpu.VMEM((ROWS, 2 * PAIR), BF), pltpu.VMEM((ROWS, 3 * FFW), BF)]
        + semaphores(7),
    )
    sums = lax.psum_scatter(parts, "y", scatter_dimension=0, tiled=True)

    rows, ids, gates, _ = lax.optimization_barrier((rows, ids, gates, parts))
    pick, gated = call(
        table_kernel,
        [shape(2, ROWS, tokens.shape[0])] * 2,
        ids,
        gates,
    )
    own, other = split_features(core, rows)
    other = swap(other)
    own, other = own.reshape(N_Y, SHARD, PAIR), other.reshape(N_Y, SHARD, PAIR)
    cut = SHARD - PIECE
    own_last = own[:, cut:].reshape(QROWS, PAIR)
    other_last = other[:, cut:].reshape(QROWS, PAIR)
    first = jnp.where(core == 0, own, other)[:, None, :cut]
    second = jnp.where(core == 0, other, own)[:, None, :cut]
    main = jnp.concatenate([first, second], axis=1).reshape(2 * MAIN * QROWS, PAIR)
    sums, main, own_last, other_last, pick, gated = lax.optimization_barrier(
        (sums, main, own_last, other_last, pick, gated)
    )

    shard_shape = shape(cut, 3 * FFW)
    shard, shard_last = call(
        shard_kernel,
        [pltpu.HBM((cut, 3 * FFW), BF), shape(PIECE, 3 * FFW)],
        *in_hbm(sums),
        in_specs=[HBM_SPEC],
        out_specs=[HBM_SPEC, VMEM_SPEC],
        scratch_shapes=buffers(sums, shard_shape) + semaphores(1, 1),
    )
    full = lax.all_gather(shard, ("y", "core"), axis=0, tiled=True)

    full_last = lax.all_gather(shard_last, "y", axis=0, tiled=True)
    send_last = call(
        back_last_kernel, shape(EXPERTS, 1, QUAD, 2 * PAIR), full_last, *in_vmem(*stacks)
    )
    back_last = across(send_last, "expert")
    full_other = swap(after(full_last, send_last))

    back = call(
        back_kernel,
        shape(EXPERTS, MAIN, QUAD, 2 * PAIR),
        *in_hbm(full, gate_own, up_own, down_own),
        in_specs=[HBM_SPEC] * 4,
        out_specs=VMEM_SPEC,
        scratch_shapes=[
            pltpu.VMEM((2, MAIN * QROWS, 3 * FFW), BF),
            pltpu.VMEM((3, WIDE, FFW), BF),
        ]
        + semaphores(3 + 2 * N_Y),
    )
    grad_inputs = (full, full_last, full_other, after(main, back), own_last, other_last)
    grads = call(
        grads_kernel,
        [shape(WIDE, FFW)] * 3,
        *in_hbm(*grad_inputs),
        in_specs=[HBM_SPEC] * 6,
        scratch_shapes=buffers(*grad_inputs) + semaphores(8),
    )
    back = across(back, "expert")
    back_last = after(back_last, grads[2])
    total_last = call(
        mix_last_kernel,
        shape(tokens.shape[0], 2 * PAIR, dtype=F32),
        core.reshape(1),
        pick,
        gated,
        back_last,
        in_specs=[SMEM_SPEC] + [VMEM_SPEC] * 3,
    )
    other_total = swap(total_last)
    back = after(back, other_total, *grads)
    token_grad, mixed = call(
        mix_kernel,
        [shape(*tokens.shape)] * 2,
        core.reshape(1),
        pick,
        gated,
        back,
        total_last,
        other_total,
        in_specs=[SMEM_SPEC] + [VMEM_SPEC] * 5,
    )
    return mixed, token_grad, grads[0][None], grads[1][None], grads[2].T[None]


def solution(mesh):
    fine = Mesh(mesh.devices.reshape(N_Y, 2, EXPERTS), ("y", "core", "expert"))
    dp = ("y", "core")
    placed = (
        P("expert", dp),
        P("expert", None),
        P("expert", None),
        P("expert", dp, None),
        P("expert", dp, None),
        P("expert", None, dp),
        P("expert", dp),
    )
    return jax.shard_map(
        body,
        mesh=fine,
        in_specs=placed,
        out_specs=(
            P("expert", dp),
            P("expert", dp),
            P("expert", dp, None),
            P("expert", dp, None),
            P("expert", None, dp),
        ),
        check_vma=False,
    )
```

```python
import jax
import jax.numpy as jnp
from jax import lax
from jax.experimental import pallas as pl
from jax.experimental.pallas import tpu as pltpu
from jax.sharding import Mesh, PartitionSpec as P

EXPERTS = 32
CAP = 32
HALF = CAP // 2
QUAD = 4
QUADS = HALF // QUAD
MAIN = QUADS - 1
QROWS = EXPERTS * QUAD
ROWS = QUADS * QROWS
WIDE = 224
PAIR = 2 * WIDE
STACK = 512
JOIN = 2 * PAIR - STACK
FFW = 1024
N_Y = 8
PIECE = QROWS // N_Y
SHARD = ROWS // N_Y
BF = jnp.bfloat16
F32 = jnp.float32
VMEM_LIMIT = 24 * 1024 * 1024


def iota(shape, dim):
    return lax.broadcasted_iota(jnp.int32, shape, dim)


def dot(left, right):
    return jnp.dot(left, right, preferred_element_type=F32)


def dot_t(left, right):
    return lax.dot_general(left, right, (((1,), (1,)), ((), ())), preferred_element_type=F32)


def t_dot(left, right):
    return lax.dot_general(left, right, (((0,), (0,)), ((), ())), preferred_element_type=F32)


def shape(*dims, dtype=BF):
    return jax.ShapeDtypeStruct(dims, dtype)


def start(copies):
    for copy in copies:
        copy.start()


def wait(copies):
    for copy in copies:
        copy.wait()


def copies_of(pairs, sems):
    return [pltpu.make_async_copy(src, dst, sems.at[i]) for i, (src, dst) in enumerate(pairs)]


def slot_table(ids_ref, gates_ref, firsts):
    tokens = ids_ref.shape[1]
    numbers = iota((EXPERTS, tokens), 0)
    chosen = jnp.zeros((EXPERTS, tokens), F32)
    weight = jnp.zeros((EXPERTS, tokens), F32)
    for k in range(ids_ref.shape[0]):
        hit = ids_ref[k : k + 1, :] == numbers
        chosen = chosen + jnp.where(hit, 1.0, 0.0)
        weight = weight + jnp.where(hit, gates_ref[k : k + 1, :], 0.0)
    earlier = jnp.where(iota((tokens, tokens), 0) < iota((tokens, tokens), 1), 1.0, 0.0)
    rank = dot(chosen.astype(BF), earlier.astype(BF))
    rank = jnp.where(chosen > 0.5, rank, -1.0).astype(jnp.int32)
    tables = []
    for first in firsts:
        hit = (rank - first)[:, None, :] == iota((EXPERTS, QUAD, tokens), 1)
        pick = jnp.where(hit, 1.0, 0.0).reshape(QROWS, tokens)
        gate = jnp.where(hit, weight[:, None, :], 0.0).reshape(QROWS, tokens)
        tables.append((pick.astype(BF), jnp.sum(gate, axis=1, keepdims=True)))
    return tables


def send_kernel(
    ids_hbm,
    gates_hbm,
    tokens_hbm,
    cotangent_hbm,
    out_ref,
    ids_ref,
    gates_ref,
    tokens_ref,
    cotangent_ref,
    sems,
):
    loads = copies_of(
        (
            (ids_hbm, ids_ref),
            (gates_hbm, gates_ref),
            (tokens_hbm, tokens_ref),
            (cotangent_hbm, cotangent_ref),
        ),
        sems,
    )
    start(loads)
    wait(loads[:2])
    tables = slot_table(ids_ref, gates_ref, [QUAD * q for q in range(2 * QUADS)])
    wait(loads[2:])
    features = jnp.concatenate([tokens_ref[...], cotangent_ref[...]], axis=1)
    for pair in range(QUADS):
        rows = []
        for pick, gate in tables[2 * pair : 2 * pair + 2]:
            scale = jnp.where(iota((1, PAIR), 1) < WIDE, 1.0, gate)
            rows.append(dot(pick, features) * scale)
        rows = jnp.concatenate(rows, axis=1).reshape(EXPERTS, QUAD, 2 * PAIR)
        half, place = pair // (QUADS // 2), pair % (QUADS // 2)
        out_ref[half * EXPERTS : (half + 1) * EXPERTS, place] = rows.astype(BF)


def table_kernel(ids_ref, gates_ref, pick_ref, gated_ref):
    firsts = [QUAD * q for q in range(2 * QUADS)]
    for i, (pick, gate) in enumerate(slot_table(ids_ref, gates_ref, firsts)):
        half, q = i // QUADS, i % QUADS
        pick_ref[half, q * QROWS : (q + 1) * QROWS] = pick
        gated_ref[half, q * QROWS : (q + 1) * QROWS] = (pick.astype(F32) * gate).astype(BF)


def sums_kernel(quads, gate, up, down, rows_hbm, out_hbm, rows, out, sems):
    wide = FFW // 2
    columns = [pl.ds(i * wide, wide) for i in range(6)]
    stores = copies_of([(out.at[:, c], out_hbm.at[:, c]) for c in columns], sems)
    for q in range(QUADS):
        pieces = []
        for core in range(2):
            block = quads[core * EXPERTS : (core + 1) * EXPERTS, q // 2].astype(F32)
            block = block.reshape(QROWS, 2 * PAIR)[:, q % 2 * PAIR : (q % 2 + 1) * PAIR]
            pieces.append((block[:, :WIDE], block[:, WIDE:]))
        (in_0, dy_0), (in_1, dy_1) = pieces
        block = jnp.concatenate([in_0, in_1, dy_0, dy_1], axis=1).astype(BF)
        for y in range(N_Y):
            at = y * SHARD + q * PIECE
            rows[at : at + PIECE] = block[y * PIECE : (y + 1) * PIECE]
    rows_store = pltpu.make_async_copy(rows, rows_hbm, sems.at[6])
    rows_store.start()
    for i, weights in enumerate((gate, gate, up, up, down, down)):
        left = rows[:, :STACK] if i < 4 else rows[:, 2 * PAIR - STACK :]
        right = weights[:, i % 2 * wide : (i % 2 + 1) * wide]
        out[:, i * wide : (i + 1) * wide] = dot(left, right).astype(BF)
        stores[i].start()
    wait(stores + [rows_store])


def shard_kernel(sums_hbm, main_hbm, last_ref, sums, main, in_sem, out_sem):
    load = pltpu.make_async_copy(sums_hbm, sums, in_sem.at[0])
    store = pltpu.make_async_copy(main, main_hbm, out_sem.at[0])
    load.start()
    load.wait()
    gate_sum, up_sum, total = [sums[:, i * FFW : (i + 1) * FFW].astype(F32) for i in range(3)]
    logistic = jax.nn.sigmoid(gate_sum)
    silu = gate_sum * logistic
    slope = logistic * (1.0 + gate_sum * (1.0 - logistic))
    results = [silu * up_sum, total * up_sum * slope, total * silu]
    cut = SHARD - PIECE
    for i, result in enumerate(results):
        main[:, i * FFW : (i + 1) * FFW] = result[:cut].astype(BF)
    store.start()
    for i, result in enumerate(results):
        last_ref[:, i * FFW : (i + 1) * FFW] = result[cut:].astype(BF)
    store.wait()


def back_parts(full, weights):
    grad = dot_t(full[:, FFW : 2 * FFW], weights[1]) + dot_t(full[:, 2 * FFW :], weights[2])
    return [grad, dot_t(full[:, :FFW], weights[0])]


def back_kernel(full_hbm, gate_hbm, up_hbm, down_hbm, out_ref, full, weights, sems):
    size = full.shape[1] // N_Y
    loads = copies_of(
        [(w, weights.at[i]) for i, w in enumerate((down_hbm, gate_hbm, up_hbm))]
        + [
            (full_hbm.at[pl.ds((2 * y + half) * size, size)], full.at[half, pl.ds(y * size, size)])
            for half in range(2)
            for y in range(N_Y)
        ],
        sems,
    )
    start(loads)
    wait(loads[:3])
    parts = []
    for half in range(2):
        wait(loads[3 + half * N_Y : 3 + (half + 1) * N_Y])
        parts += back_parts(full.at[half], weights)
    result = jnp.concatenate(parts, axis=1)
    for q in range(MAIN):
        starts = [y * size + q * PIECE for y in range(N_Y)]
        block = jnp.concatenate([result[at : at + PIECE] for at in starts], axis=0)
        out_ref[:, q] = block.reshape(EXPERTS, QUAD, 2 * PAIR).astype(BF)


def back_last_kernel(full, gate, up, down, out_ref):
    result = dot_t(full[:, :FFW], down[...])
    grad = dot_t(full[:, FFW : 2 * FFW], gate[...]) + dot_t(full[:, 2 * FFW :], up[...])
    middle = grad[:, JOIN:] + result[:, : STACK - JOIN]
    rows = jnp.concatenate([grad[:, :JOIN], middle, result[:, STACK - JOIN :]], axis=1)
    out_ref[:, 0] = rows.reshape(EXPERTS, QUAD, 2 * PAIR).astype(BF)


def grads_kernel(*refs):
    hbm, (gate_ref, up_ref, down_ref), bufs, sems = refs[:6], refs[6:9], refs[9:15], refs[15]
    full_hbm, full = hbm[0], bufs[0]
    columns = [pl.ds(i * FFW, FFW) for i in range(3)]
    pairs = list(zip(hbm[1:], bufs[1:])) + [(full_hbm.at[:, c], full.at[:, c]) for c in columns]
    loads = copies_of(pairs, sems)
    start(loads)
    wait(loads[:5])
    for i, (out, first) in enumerate(((down_ref, WIDE), (gate_ref, 0), (up_ref, 0))):
        loads[5 + i].wait()
        total = 0.0
        for sums, rows in zip(bufs[:3], bufs[3:]):
            total = total + t_dot(rows[:, first : first + WIDE], sums[:, columns[i]])
        out[...] = total.astype(BF)


def mix_last_kernel(core_ref, pick_ref, gated_ref, last_ref, out_ref):
    back = last_ref[:, 0].astype(F32).reshape(QROWS, 2 * PAIR).astype(BF)
    rows = pl.ds(MAIN * QROWS, QROWS)
    plain = t_dot(pick_ref[core_ref[0], rows], back)
    gated = t_dot(gated_ref[core_ref[0], rows], back)
    out_ref[...] = jnp.where(iota((1, 2 * PAIR), 1) < PAIR, plain, gated)


def mix_kernel(core_ref, pick_ref, gated_ref, main_ref, own_ref, other_ref, grad_ref, mixed_ref):
    quads = [main_ref[:, q] for q in range(MAIN)]
    quads = [q.astype(F32).reshape(QROWS, 2 * PAIR).astype(BF) for q in quads]
    back = jnp.concatenate(quads, axis=0)
    rows = slice(0, MAIN * QROWS)
    totals = []
    for half in range(2):
        columns = back[:, half * JOIN : half * JOIN + STACK]
        plain = t_dot(pick_ref[half, rows], columns)
        gated = t_dot(gated_ref[half, rows], columns)
        skip = half * (PAIR - JOIN)
        totals.append(jnp.where(iota((1, STACK), 1) < skip + WIDE, plain, gated))
    total = totals[0][:, :PAIR] + totals[1][:, STACK - PAIR :]
    last = own_ref[...] + other_ref[...]
    is_first = core_ref[0] == 0
    grad = total[:, :WIDE] + jnp.where(is_first, last[:, :WIDE], last[:, WIDE:PAIR])
    last = jnp.where(is_first, last[:, PAIR : PAIR + WIDE], last[:, PAIR + WIDE :])
    grad_ref[...] = grad.astype(BF)
    mixed_ref[...] = (total[:, WIDE:] + last).astype(BF)


HBM_SPEC = pl.BlockSpec(memory_space=pltpu.HBM)
VMEM_SPEC = pl.BlockSpec(memory_space=pltpu.VMEM)
SMEM_SPEC = pl.BlockSpec(memory_space=pltpu.SMEM)


def call(kernel, out_shape, *args, **kwargs):
    return pl.pallas_call(
        kernel,
        out_shape=out_shape,
        compiler_params=pltpu.CompilerParams(vmem_limit_bytes=VMEM_LIMIT),
        name=kernel.__name__,
        **kwargs,
    )(*args)


def in_hbm(*arrays):
    return [pltpu.with_memory_space_constraint(a, pltpu.HBM) for a in arrays]


def in_vmem(*arrays):
    return [pltpu.with_memory_space_constraint(a, pltpu.VMEM) for a in arrays]


def buffers(*arrays):
    return [pltpu.VMEM(a.shape, a.dtype) for a in arrays]


def semaphores(*counts):
    return [pltpu.SemaphoreType.DMA((n,)) for n in counts]


def across(quads, axis):
    return lax.all_to_all(quads, axis, split_axis=0, concat_axis=0, tiled=True)


def swap(array):
    return lax.ppermute(array, "core", [(0, 1), (1, 0)])


def after(array, *others):
    return lax.optimization_barrier((array,) + others)[0]


def by_core(core, own, other):
    return jnp.where(core == 0, own, other), jnp.where(core == 0, other, own)


def split_features(core, rows):
    first = jnp.concatenate([rows[:, :WIDE], rows[:, PAIR : PAIR + WIDE]], axis=1)
    second = jnp.concatenate([rows[:, WIDE:PAIR], rows[:, PAIR + WIDE :]], axis=1)
    return by_core(core, first, second)


def body(tokens, expert_ids, gate_weights, w_gate, w_up, w_down, cotangent):
    gate_own, up_own, down_own = w_gate[0], w_up[0], w_down[0].T
    core = lax.axis_index("core")
    ids, gates = expert_ids.T, gate_weights.T
    inputs = (ids, gates, tokens, cotangent)
    send = call(
        send_kernel,
        shape(2 * EXPERTS, QUADS // 2, QUAD, 2 * PAIR),
        *in_hbm(*inputs),
        in_specs=[HBM_SPEC] * 4,
        scratch_shapes=buffers(*inputs) + semaphores(4),
    )
    quads = across(send, ("core", "expert"))
    gate_sent, up_sent, down_sent, _ = lax.optimization_barrier((gate_own, up_own, down_own, send))
    zeros = jnp.zeros((STACK - PAIR, FFW), BF)
    stacks = (
        jnp.concatenate([*by_core(core, gate_sent, swap(gate_sent)), zeros], axis=0),
        jnp.concatenate([*by_core(core, up_sent, swap(up_sent)), zeros], axis=0),
        jnp.concatenate([zeros, *by_core(core, down_sent, swap(down_sent))], axis=0),
    )
    rows, parts = call(
        sums_kernel,
        [pltpu.HBM((ROWS, 2 * PAIR), BF), pltpu.HBM((ROWS, 3 * FFW), BF)],
        quads,
        *in_vmem(*stacks),
        in_specs=[VMEM_SPEC] * 4,
        out_specs=[HBM_SPEC] * 2,
        scratch_shapes=[pltpu.VMEM((ROWS, 2 * PAIR), BF), pltpu.VMEM((ROWS, 3 * FFW), BF)]
        + semaphores(7),
    )
    sums = lax.psum_scatter(parts, "y", scatter_dimension=0, tiled=True)

    rows, ids, gates, _ = lax.optimization_barrier((rows, ids, gates, parts))
    pick, gated = call(
        table_kernel,
        [shape(2, ROWS, tokens.shape[0])] * 2,
        ids,
        gates,
    )
    own, other = split_features(core, rows)
    other = swap(other)
    own, other = own.reshape(N_Y, SHARD, PAIR), other.reshape(N_Y, SHARD, PAIR)
    cut = SHARD - PIECE
    own_last = own[:, cut:].reshape(QROWS, PAIR)
    other_last = other[:, cut:].reshape(QROWS, PAIR)
    first = jnp.where(core == 0, own, other)[:, None, :cut]
    second = jnp.where(core == 0, other, own)[:, None, :cut]
    main = jnp.concatenate([first, second], axis=1).reshape(2 * MAIN * QROWS, PAIR)
    sums, main, own_last, other_last, pick, gated = lax.optimization_barrier(
        (sums, main, own_last, other_last, pick, gated)
    )

    shard_shape = shape(cut, 3 * FFW)
    shard, shard_last = call(
        shard_kernel,
        [pltpu.HBM((cut, 3 * FFW), BF), shape(PIECE, 3 * FFW)],
        *in_hbm(sums),
        in_specs=[HBM_SPEC],
        out_specs=[HBM_SPEC, VMEM_SPEC],
        scratch_shapes=buffers(sums, shard_shape) + semaphores(1, 1),
    )
    full = lax.all_gather(shard, ("y", "core"), axis=0, tiled=True)

    full_last = lax.all_gather(shard_last, "y", axis=0, tiled=True)
    send_last = call(
        back_last_kernel, shape(EXPERTS, 1, QUAD, 2 * PAIR), full_last, *in_vmem(*stacks)
    )
    back_last = across(send_last, "expert")
    full_other = swap(after(full_last, send_last))
    full, full_other = lax.optimization_barrier((full, full_other))

    back = call(
        back_kernel,
        shape(EXPERTS, MAIN, QUAD, 2 * PAIR),
        *in_hbm(full, gate_own, up_own, down_own),
        in_specs=[HBM_SPEC] * 4,
        out_specs=VMEM_SPEC,
        scratch_shapes=[
            pltpu.VMEM((2, MAIN * QROWS, 3 * FFW), BF),
            pltpu.VMEM((3, WIDE, FFW), BF),
        ]
        + semaphores(3 + 2 * N_Y),
    )
    grad_inputs = (full, full_last, full_other, after(main, back), own_last, other_last)
    grads = call(
        grads_kernel,
        [shape(WIDE, FFW)] * 3,
        *in_hbm(*grad_inputs),
        in_specs=[HBM_SPEC] * 6,
        scratch_shapes=buffers(*grad_inputs) + semaphores(8),
    )
    back = across(back, "expert")
    back_last = after(back_last, grads[2])
    total_last = call(
        mix_last_kernel,
        shape(tokens.shape[0], 2 * PAIR, dtype=F32),
        core.reshape(1),
        pick,
        gated,
        back_last,
        in_specs=[SMEM_SPEC] + [VMEM_SPEC] * 3,
    )
    other_total = swap(total_last)
    back = after(back, other_total, *grads)
    token_grad, mixed = call(
        mix_kernel,
        [shape(*tokens.shape)] * 2,
        core.reshape(1),
        pick,
        gated,
        back,
        total_last,
        other_total,
        in_specs=[SMEM_SPEC] + [VMEM_SPEC] * 5,
    )
    return mixed, token_grad, grads[0][None], grads[1][None], grads[2].T[None]


def solution(mesh):
    fine = Mesh(mesh.devices.reshape(N_Y, 2, EXPERTS), ("y", "core", "expert"))
    dp = ("y", "core")
    placed = (
        P("expert", dp),
        P("expert", None),
        P("expert", None),
        P("expert", dp, None),
        P("expert", dp, None),
        P("expert", None, dp),
        P("expert", dp),
    )
    return jax.shard_map(
        body,
        mesh=fine,
        in_specs=placed,
        out_specs=(
            P("expert", dp),
            P("expert", dp),
            P("expert", dp, None),
            P("expert", dp, None),
            P("expert", None, dp),
        ),
        check_vma=False,
    )
```

```python
import jax
import jax.numpy as jnp
from jax import lax
from jax.experimental import pallas as pl
from jax.experimental.pallas import tpu as pltpu
from jax.sharding import Mesh, PartitionSpec as P

EXPERTS = 32
CAP = 32
HALF = CAP // 2
QUAD = 4
QUADS = HALF // QUAD
MAIN = QUADS - 1
QROWS = EXPERTS * QUAD
ROWS = QUADS * QROWS
WIDE = 224
PAIR = 2 * WIDE
STACK = 512
JOIN = 2 * PAIR - STACK
FFW = 1024
N_Y = 8
PIECE = QROWS // N_Y
SHARD = ROWS // N_Y
BF = jnp.bfloat16
F32 = jnp.float32
VMEM_LIMIT = 24 * 1024 * 1024


def iota(shape, dim):
    return lax.broadcasted_iota(jnp.int32, shape, dim)


def dot(left, right):
    return jnp.dot(left, right, preferred_element_type=F32)


def dot_t(left, right):
    return lax.dot_general(left, right, (((1,), (1,)), ((), ())), preferred_element_type=F32)


def t_dot(left, right):
    return lax.dot_general(left, right, (((0,), (0,)), ((), ())), preferred_element_type=F32)


def shape(*dims, dtype=BF):
    return jax.ShapeDtypeStruct(dims, dtype)


def start(copies):
    for copy in copies:
        copy.start()


def wait(copies):
    for copy in copies:
        copy.wait()


def copies_of(pairs, sems):
    return [pltpu.make_async_copy(src, dst, sems.at[i]) for i, (src, dst) in enumerate(pairs)]


def slot_table(ids_ref, gates_ref, firsts):
    tokens = ids_ref.shape[1]
    numbers = iota((EXPERTS, tokens), 0)
    chosen = jnp.zeros((EXPERTS, tokens), F32)
    weight = jnp.zeros((EXPERTS, tokens), F32)
    for k in range(ids_ref.shape[0]):
        hit = ids_ref[k : k + 1, :] == numbers
        chosen = chosen + jnp.where(hit, 1.0, 0.0)
        weight = weight + jnp.where(hit, gates_ref[k : k + 1, :], 0.0)
    earlier = jnp.where(iota((tokens, tokens), 0) < iota((tokens, tokens), 1), 1.0, 0.0)
    rank = dot(chosen.astype(BF), earlier.astype(BF))
    rank = jnp.where(chosen > 0.5, rank, -1.0).astype(jnp.int32)
    tables = []
    for first in firsts:
        hit = (rank - first)[:, None, :] == iota((EXPERTS, QUAD, tokens), 1)
        pick = jnp.where(hit, 1.0, 0.0).reshape(QROWS, tokens)
        gate = jnp.where(hit, weight[:, None, :], 0.0).reshape(QROWS, tokens)
        tables.append((pick.astype(BF), jnp.sum(gate, axis=1, keepdims=True)))
    return tables


def send_kernel(
    ids_hbm,
    gates_hbm,
    tokens_hbm,
    cotangent_hbm,
    out_ref,
    ids_ref,
    gates_ref,
    tokens_ref,
    cotangent_ref,
    sems,
):
    loads = copies_of(
        (
            (ids_hbm, ids_ref),
            (gates_hbm, gates_ref),
            (tokens_hbm, tokens_ref),
            (cotangent_hbm, cotangent_ref),
        ),
        sems,
    )
    start(loads)
    wait(loads[:2])
    tables = slot_table(ids_ref, gates_ref, [QUAD * q for q in range(2 * QUADS)])
    wait(loads[2:])
    features = jnp.concatenate([tokens_ref[...], cotangent_ref[...]], axis=1)
    for pair in range(QUADS):
        rows = []
        for pick, gate in tables[2 * pair : 2 * pair + 2]:
            scale = jnp.where(iota((1, PAIR), 1) < WIDE, 1.0, gate)
            rows.append(dot(pick, features) * scale)
        rows = jnp.concatenate(rows, axis=1).reshape(EXPERTS, QUAD, 2 * PAIR)
        half, place = pair // (QUADS // 2), pair % (QUADS // 2)
        out_ref[half * EXPERTS : (half + 1) * EXPERTS, place] = rows.astype(BF)


def table_kernel(ids_ref, gates_ref, pick_ref, gated_ref):
    firsts = [QUAD * q for q in range(2 * QUADS)]
    for i, (pick, gate) in enumerate(slot_table(ids_ref, gates_ref, firsts)):
        half, q = i // QUADS, i % QUADS
        pick_ref[half, q * QROWS : (q + 1) * QROWS] = pick
        gated_ref[half, q * QROWS : (q + 1) * QROWS] = (pick.astype(F32) * gate).astype(BF)


def sums_kernel(quads, gate, up, down, rows_hbm, out_hbm, rows, out, sems):
    wide = FFW // 2
    columns = [pl.ds(i * wide, wide) for i in range(6)]
    stores = copies_of([(out.at[:, c], out_hbm.at[:, c]) for c in columns], sems)
    for q in range(QUADS):
        pieces = []
        for core in range(2):
            block = quads[core * EXPERTS : (core + 1) * EXPERTS, q // 2].astype(F32)
            block = block.reshape(QROWS, 2 * PAIR)[:, q % 2 * PAIR : (q % 2 + 1) * PAIR]
            pieces.append((block[:, :WIDE], block[:, WIDE:]))
        (in_0, dy_0), (in_1, dy_1) = pieces
        block = jnp.concatenate([in_0, in_1, dy_0, dy_1], axis=1).astype(BF)
        for y in range(N_Y):
            at = y * SHARD + q * PIECE
            rows[at : at + PIECE] = block[y * PIECE : (y + 1) * PIECE]
    rows_store = pltpu.make_async_copy(rows, rows_hbm, sems.at[6])
    rows_store.start()
    for i, weights in enumerate((gate, gate, up, up, down, down)):
        left = rows[:, :STACK] if i < 4 else rows[:, 2 * PAIR - STACK :]
        right = weights[:, i % 2 * wide : (i % 2 + 1) * wide]
        out[:, i * wide : (i + 1) * wide] = dot(left, right).astype(BF)
        stores[i].start()
    wait(stores + [rows_store])


def shard_kernel(sums_hbm, main_hbm, last_ref, sums, main, in_sem, out_sem):
    load = pltpu.make_async_copy(sums_hbm, sums, in_sem.at[0])
    store = pltpu.make_async_copy(main, main_hbm, out_sem.at[0])
    load.start()
    load.wait()
    gate_sum, up_sum, total = [sums[:, i * FFW : (i + 1) * FFW].astype(F32) for i in range(3)]
    logistic = jax.nn.sigmoid(gate_sum)
    silu = gate_sum * logistic
    slope = logistic * (1.0 + gate_sum * (1.0 - logistic))
    results = [silu * up_sum, total * up_sum * slope, total * silu]
    cut = SHARD - PIECE
    for i, result in enumerate(results):
        main[:, i * FFW : (i + 1) * FFW] = result[:cut].astype(BF)
    store.start()
    for i, result in enumerate(results):
        last_ref[:, i * FFW : (i + 1) * FFW] = result[cut:].astype(BF)
    store.wait()


def back_kernel(full_hbm, gate_hbm, up_hbm, down_hbm, out_ref, full, weights, sems):
    size = full.shape[1] // N_Y
    pairs = [
        (full_hbm.at[pl.ds((2 * y + half) * size, size)], full.at[half, pl.ds(y * size, size)])
        for half in range(2)
        for y in range(N_Y)
    ]
    inner = [(w, weights.at[i]) for i, w in enumerate((gate_hbm, up_hbm, down_hbm))]
    loads = copies_of(pairs[:N_Y] + inner + pairs[N_Y:], sems)
    start(loads)
    parts = []
    for half in range(2):
        first = half * (N_Y + 3)
        wait(loads[first : first + N_Y])
        products = []
        for i, column in enumerate((1, 2, 0)):
            if half == 0:
                loads[N_Y + i].wait()
            rows = full[half, :, column * FFW : (column + 1) * FFW]
            products.append(dot_t(rows, weights[i]))
        parts += [products[0] + products[1], products[2]]
    result = jnp.concatenate(parts, axis=1)
    for q in range(MAIN):
        starts = [y * size + q * PIECE for y in range(N_Y)]
        block = jnp.concatenate([result[at : at + PIECE] for at in starts], axis=0)
        out_ref[:, q] = block.reshape(EXPERTS, QUAD, 2 * PAIR).astype(BF)


def back_last_kernel(full, gate, up, down, out_ref):
    result = dot_t(full[:, :FFW], down[...])
    grad = dot_t(full[:, FFW : 2 * FFW], gate[...]) + dot_t(full[:, 2 * FFW :], up[...])
    middle = grad[:, JOIN:] + result[:, : STACK - JOIN]
    rows = jnp.concatenate([grad[:, :JOIN], middle, result[:, STACK - JOIN :]], axis=1)
    out_ref[:, 0] = rows.reshape(EXPERTS, QUAD, 2 * PAIR).astype(BF)


def grads_kernel(*refs):
    hbm, (gate_ref, up_ref, down_ref), bufs, sems = refs[:6], refs[6:9], refs[9:15], refs[15]
    full_hbm, full = hbm[0], bufs[0]
    columns = [pl.ds(i * FFW, FFW) for i in range(3)]
    pairs = list(zip(hbm[1:], bufs[1:])) + [(full_hbm.at[:, c], full.at[:, c]) for c in columns]
    loads = copies_of(pairs, sems)
    start(loads)
    wait(loads[:5])
    for i, (out, first) in enumerate(((down_ref, WIDE), (gate_ref, 0), (up_ref, 0))):
        loads[5 + i].wait()
        total = 0.0
        for sums, rows in zip(bufs[:3], bufs[3:]):
            total = total + t_dot(rows[:, first : first + WIDE], sums[:, columns[i]])
        out[...] = total.astype(BF)


def mix_last_kernel(core_ref, pick_ref, gated_ref, last_ref, out_ref):
    back = last_ref[:, 0].astype(F32).reshape(QROWS, 2 * PAIR).astype(BF)
    rows = pl.ds(MAIN * QROWS, QROWS)
    plain = t_dot(pick_ref[core_ref[0], rows], back)
    gated = t_dot(gated_ref[core_ref[0], rows], back)
    out_ref[...] = jnp.where(iota((1, 2 * PAIR), 1) < PAIR, plain, gated)


def mix_kernel(core_ref, pick_ref, gated_ref, main_ref, own_ref, other_ref, grad_ref, mixed_ref):
    quads = [main_ref[:, q] for q in range(MAIN)]
    quads = [q.astype(F32).reshape(QROWS, 2 * PAIR).astype(BF) for q in quads]
    back = jnp.concatenate(quads, axis=0)
    rows = slice(0, MAIN * QROWS)
    totals = []
    for half in range(2):
        columns = back[:, half * JOIN : half * JOIN + STACK]
        plain = t_dot(pick_ref[half, rows], columns)
        gated = t_dot(gated_ref[half, rows], columns)
        skip = half * (PAIR - JOIN)
        totals.append(jnp.where(iota((1, STACK), 1) < skip + WIDE, plain, gated))
    total = totals[0][:, :PAIR] + totals[1][:, STACK - PAIR :]
    last = own_ref[...] + other_ref[...]
    is_first = core_ref[0] == 0
    grad = total[:, :WIDE] + jnp.where(is_first, last[:, :WIDE], last[:, WIDE:PAIR])
    last = jnp.where(is_first, last[:, PAIR : PAIR + WIDE], last[:, PAIR + WIDE :])
    grad_ref[...] = grad.astype(BF)
    mixed_ref[...] = (total[:, WIDE:] + last).astype(BF)


HBM_SPEC = pl.BlockSpec(memory_space=pltpu.HBM)
VMEM_SPEC = pl.BlockSpec(memory_space=pltpu.VMEM)
SMEM_SPEC = pl.BlockSpec(memory_space=pltpu.SMEM)


def call(kernel, out_shape, *args, **kwargs):
    return pl.pallas_call(
        kernel,
        out_shape=out_shape,
        compiler_params=pltpu.CompilerParams(vmem_limit_bytes=VMEM_LIMIT),
        name=kernel.__name__,
        **kwargs,
    )(*args)


def in_hbm(*arrays):
    return [pltpu.with_memory_space_constraint(a, pltpu.HBM) for a in arrays]


def in_vmem(*arrays):
    return [pltpu.with_memory_space_constraint(a, pltpu.VMEM) for a in arrays]


def buffers(*arrays):
    return [pltpu.VMEM(a.shape, a.dtype) for a in arrays]


def semaphores(*counts):
    return [pltpu.SemaphoreType.DMA((n,)) for n in counts]


def across(quads, axis):
    return lax.all_to_all(quads, axis, split_axis=0, concat_axis=0, tiled=True)


def swap(array):
    return lax.ppermute(array, "core", [(0, 1), (1, 0)])


def after(array, *others):
    return lax.optimization_barrier((array,) + others)[0]


def by_core(core, own, other):
    return jnp.where(core == 0, own, other), jnp.where(core == 0, other, own)


def split_features(core, rows):
    first = jnp.concatenate([rows[:, :WIDE], rows[:, PAIR : PAIR + WIDE]], axis=1)
    second = jnp.concatenate([rows[:, WIDE:PAIR], rows[:, PAIR + WIDE :]], axis=1)
    return by_core(core, first, second)


def body(tokens, expert_ids, gate_weights, w_gate, w_up, w_down, cotangent):
    gate_own, up_own, down_own = w_gate[0], w_up[0], w_down[0].T
    core = lax.axis_index("core")
    ids, gates = expert_ids.T, gate_weights.T
    inputs = (ids, gates, tokens, cotangent)
    send = call(
        send_kernel,
        shape(2 * EXPERTS, QUADS // 2, QUAD, 2 * PAIR),
        *in_hbm(*inputs),
        in_specs=[HBM_SPEC] * 4,
        scratch_shapes=buffers(*inputs) + semaphores(4),
    )
    quads = across(send, ("core", "expert"))
    gate_sent, up_sent, down_sent, _ = lax.optimization_barrier((gate_own, up_own, down_own, send))
    zeros = jnp.zeros((STACK - PAIR, FFW), BF)
    stacks = (
        jnp.concatenate([*by_core(core, gate_sent, swap(gate_sent)), zeros], axis=0),
        jnp.concatenate([*by_core(core, up_sent, swap(up_sent)), zeros], axis=0),
        jnp.concatenate([zeros, *by_core(core, down_sent, swap(down_sent))], axis=0),
    )
    rows, parts = call(
        sums_kernel,
        [pltpu.HBM((ROWS, 2 * PAIR), BF), pltpu.HBM((ROWS, 3 * FFW), BF)],
        quads,
        *in_vmem(*stacks),
        in_specs=[VMEM_SPEC] * 4,
        out_specs=[HBM_SPEC] * 2,
        scratch_shapes=[pltpu.VMEM((ROWS, 2 * PAIR), BF), pltpu.VMEM((ROWS, 3 * FFW), BF)]
        + semaphores(7),
    )
    sums = lax.psum_scatter(parts, "y", scatter_dimension=0, tiled=True)

    rows, ids, gates, _ = lax.optimization_barrier((rows, ids, gates, parts))
    pick, gated = call(
        table_kernel,
        [shape(2, ROWS, tokens.shape[0])] * 2,
        ids,
        gates,
    )
    own, other = split_features(core, rows)
    other = swap(other)
    own, other = own.reshape(N_Y, SHARD, PAIR), other.reshape(N_Y, SHARD, PAIR)
    cut = SHARD - PIECE
    own_last = own[:, cut:].reshape(QROWS, PAIR)
    other_last = other[:, cut:].reshape(QROWS, PAIR)
    first = jnp.where(core == 0, own, other)[:, None, :cut]
    second = jnp.where(core == 0, other, own)[:, None, :cut]
    main = jnp.concatenate([first, second], axis=1).reshape(2 * MAIN * QROWS, PAIR)
    sums, main, own_last, other_last, pick, gated = lax.optimization_barrier(
        (sums, main, own_last, other_last, pick, gated)
    )

    shard_shape = shape(cut, 3 * FFW)
    shard, shard_last = call(
        shard_kernel,
        [pltpu.HBM((cut, 3 * FFW), BF), shape(PIECE, 3 * FFW)],
        *in_hbm(sums),
        in_specs=[HBM_SPEC],
        out_specs=[HBM_SPEC, VMEM_SPEC],
        scratch_shapes=buffers(sums, shard_shape) + semaphores(1, 1),
    )
    full = lax.all_gather(shard, ("y", "core"), axis=0, tiled=True)

    full_last = lax.all_gather(shard_last, "y", axis=0, tiled=True)
    send_last = call(
        back_last_kernel, shape(EXPERTS, 1, QUAD, 2 * PAIR), full_last, *in_vmem(*stacks)
    )
    back_last = across(send_last, "expert")
    full_other = swap(after(full_last, send_last))

    back = call(
        back_kernel,
        shape(EXPERTS, MAIN, QUAD, 2 * PAIR),
        *in_hbm(full, gate_own, up_own, down_own),
        in_specs=[HBM_SPEC] * 4,
        out_specs=VMEM_SPEC,
        scratch_shapes=[
            pltpu.VMEM((2, MAIN * QROWS, 3 * FFW), BF),
            pltpu.VMEM((3, WIDE, FFW), BF),
        ]
        + semaphores(3 + 2 * N_Y),
    )
    grad_inputs = (full, full_last, full_other, after(main, back), own_last, other_last)
    grads = call(
        grads_kernel,
        [shape(WIDE, FFW)] * 3,
        *in_hbm(*grad_inputs),
        in_specs=[HBM_SPEC] * 6,
        scratch_shapes=buffers(*grad_inputs) + semaphores(8),
    )
    back = across(back, "expert")
    back_last = after(back_last, grads[2])
    total_last = call(
        mix_last_kernel,
        shape(tokens.shape[0], 2 * PAIR, dtype=F32),
        core.reshape(1),
        pick,
        gated,
        back_last,
        in_specs=[SMEM_SPEC] + [VMEM_SPEC] * 3,
    )
    other_total = swap(total_last)
    back = after(back, other_total, *grads)
    token_grad, mixed = call(
        mix_kernel,
        [shape(*tokens.shape)] * 2,
        core.reshape(1),
        pick,
        gated,
        back,
        total_last,
        other_total,
        in_specs=[SMEM_SPEC] + [VMEM_SPEC] * 5,
    )
    return mixed, token_grad, grads[0][None], grads[1][None], grads[2].T[None]


def solution(mesh):
    fine = Mesh(mesh.devices.reshape(N_Y, 2, EXPERTS), ("y", "core", "expert"))
    dp = ("y", "core")
    placed = (
        P("expert", dp),
        P("expert", None),
        P("expert", None),
        P("expert", dp, None),
        P("expert", dp, None),
        P("expert", None, dp),
        P("expert", dp),
    )
    return jax.shard_map(
        body,
        mesh=fine,
        in_specs=placed,
        out_specs=(
            P("expert", dp),
            P("expert", dp),
            P("expert", dp, None),
            P("expert", dp, None),
            P("expert", None, dp),
        ),
        check_vma=False,
    )
```
